32 devices in a mesh: dp: 8 (over z, y), shard: 4 (over x, core).
Axes of the slice: x: 2, y: 2, z: 4, core: 2. Of those that a mesh axis runs over, the one named last changes fastest.
Arguments:
- tokens: bfloat16 [4096, 1024], P(('dp', 'shard')), may hold values from -6 to 6
- out_grad: bfloat16 [4096, 1024], P(('dp', 'shard')), may hold values from -6 to 6
- dest: int32 [8, 4, 128], P(None, 'shard'), may hold values from 0 to 1023, as said below
- lengths: int32 [8, 4], P('dp'), may hold values from 1 to 384, 512 in all within a row
- classes: int32 [8, 4], P('dp'), may hold values from 0 to 999
- class_table: bfloat16 [1000, 1024], P(None, 'shard'), may hold values from -6 to 6
- w_ada: bfloat16 [2, 1024, 6144], P(None, 'shard', 'dp'), may hold values from -0.1875 to 0.1875
- w_qkv: bfloat16 [2, 1024, 3, 1024], P(None, 'dp', None, 'shard'), may hold values from -0.1875 to 0.1875
- head_scale: float32 [2, 16], P(None, 'shard'), may hold values from 2.1 to 3.2
- w_proj: bfloat16 [2, 1024, 1024], P(None, 'shard', 'dp'), may hold values from -0.5 to 0.5
- w_fc1: bfloat16 [2, 1024, 4096], P(None, 'dp', 'shard'), may hold values from -0.1875 to 0.1875
- w_fc2: bfloat16 [2, 4096, 1024], P(None, 'shard', 'dp'), may hold values from -0.09375 to 0.09375
Outputs:
- mixed: bfloat16 [4096, 1024], P(('dp', 'shard'))
- tokens_grad: bfloat16 [4096, 1024], P(('dp', 'shard'))
- class_table_grad: float32 [1000, 1024], P(None, 'shard')
- w_ada_grad: float32 [2, 1024, 6144], P(None, 'shard', 'dp')
- w_qkv_grad: float32 [2, 1024, 3, 1024], P(None, 'dp', None, 'shard')
- head_scale_grad: float32 [2, 16], P(None, 'shard')
- w_proj_grad: float32 [2, 1024, 1024], P(None, 'shard', 'dp')
- w_fc1_grad: float32 [2, 1024, 4096], P(None, 'dp', 'shard')
- w_fc2_grad: float32 [2, 4096, 1024], P(None, 'shard', 'dp')
The draws below stay inside these ranges and needn't reach their ends.
Inputs may be any that keep to these rules, and one draw needn't show every extreme that they name: dest is a one-to-one map of all loader rows of shard index s onto the rows of shard index s of all packs; the loader rows of one dp index and one shard index send exactly 16 rows to each pack. The 4 lengths of a pack sum to 512; each pack has one item of exactly 384 tokens.
All inputs are finite; a program needn't handle non-finite values.
Results may differ from the reference program's by a relative error of at most 0.025.
Values may be sent and summed in bfloat16 or wider, within the bound.
No kernel may reach another device: no remote copies, remote signals or barrier semaphores. Data moves between devices by JAX's collectives and lax.ppermute only.
A program may use at most 192 MiB of HBM per device.

```python
import math
import jax
import jax.numpy as jnp
import numpy as np
from jax import lax

D = 1024
HEADS = 16
FF = 4096
NCLS = 1000
LAYERS = 2
IMAX = 4
TOK_DEV = 128
PACK = 512
TOKENS = 4096
ITEM_MOST = 384
N_DP = 8
N_SHARD = 4


def shuffle_row(sub_key):
    return jax.random.permutation(sub_key, TOK_DEV)


def draw_dest(key, part):
    key = jax.random.fold_in(key, 7)
    first_key, second_key = jax.random.split(key)
    capacity = TOK_DEV // N_DP
    dealt = jax.vmap(shuffle_row)(jax.random.split(first_key, N_DP * N_SHARD))
    dealt = dealt.astype(jnp.int32).reshape(N_DP, N_SHARD, N_DP, capacity)
    pack_ids = jnp.arange(N_DP, dtype=jnp.int32)[:, None, None, None]
    values = pack_ids * TOK_DEV + dealt
    values = jnp.transpose(values, (2, 1, 0, 3)).reshape(N_DP, N_SHARD, TOK_DEV)
    order = jax.vmap(shuffle_row)(jax.random.split(second_key, N_DP * N_SHARD))
    order = order.astype(jnp.int32).reshape(N_DP, N_SHARD, TOK_DEV)
    return jnp.take_along_axis(values, order, axis=2)


def touch_ends(drawn, key, least, high):
    longest = drawn.shape.index(max(drawn.shape))
    spots = []
    for shift in (0, 1):
        where = [jax.random.randint(jax.random.fold_in(key, axis), (), 0, length) for axis, length in enumerate(drawn.shape)]
        where[longest] = (where[longest] + shift) % drawn.shape[longest]
        spots.append(tuple(where))
    return drawn.at[spots[0]].set(least).at[spots[1]].set(high)


def level_of(key, extent, cuts, least, high):
    def one(position, blocks):
        heights = jax.random.uniform(jax.random.fold_in(jax.random.fold_in(key, 6), position), (blocks,), jnp.float32, least / len(cuts), high / len(cuts))
        return jnp.repeat(jnp.exp(heights), extent[position] // blocks).reshape((-1,) + (1,) * (len(extent) - position - 1))

    loudness = one(*cuts[0])
    for cut in cuts[1:]:
        loudness = loudness * one(*cut)
    return loudness


def profile(number_of, total, bound, lean):
    loads = [(1 << 20) // math.isqrt(grade ** lean) + 1 for grade in range(2, number_of + 1)]
    rest, holding = total - bound - (number_of - 1), [1] * (number_of - 1)
    while rest > 0:
        movable = [i for i in range(number_of - 1) if holding[i] < bound]
        pool, left = sum([loads[i] for i in movable]), rest
        for i in movable:
            more = min(bound - holding[i], max(1, left * loads[i] // pool), rest)
            holding[i] = holding[i] + more
            rest = rest - more
    return np.array([bound] + holding)


def uneven_parts(stream_key, amount, total, reach, slope):
    if amount == 2:
        one = jax.random.randint(stream_key, (), max(1, total - reach), min(reach, total - 1) + 1)
        return jnp.stack([one, total - one])
    sizes = jnp.asarray(profile(amount, total, reach, slope), jnp.int32)
    pairs = (amount - 1) // 2
    source_of, taker = sizes[1:1 + 2 * pairs:2], sizes[2:2 + 2 * pairs:2]
    room = jnp.minimum(source_of - 1, reach - taker)
    passed = jax.random.randint(jax.random.fold_in(stream_key, 1), (pairs,), 0, 1 << 20) % (room + 1)
    sizes = sizes.at[1:1 + 2 * pairs:2].set(source_of - passed).at[2:2 + 2 * pairs:2].set(taker + passed)
    return sizes[jax.random.permutation(jax.random.fold_in(stream_key, 2), amount)]


def scatter_about(stream_key, dims, scale, limit, cuts=(), kind=jnp.bfloat16):
    values = scale * jax.random.normal(stream_key, dims, jnp.float32)
    if cuts:
        values = values * level_of(stream_key, dims, cuts, -0.22, 0.18)
    return jnp.clip(values, -limit, limit).astype(kind)


def setup_inputs(seed: int = 0) -> dict:
    streams_of = jax.random.split(jax.random.key(seed), 13)
    tokens = scatter_about(streams_of[0], (TOKENS, D), 1.0, 6.0, ((0, 32),))
    out_grad = scatter_about(streams_of[1], (TOKENS, D), 1.0, 6.0, ((0, 32),))
    dest = draw_dest(jax.random.fold_in(streams_of[12], 71), 0)
    lengths = jax.vmap(lambda own: uneven_parts(own, IMAX, PACK, ITEM_MOST, 2))(jax.random.split(streams_of[3], N_DP)).reshape((N_DP, IMAX)).astype(jnp.int32)
    classes = touch_ends(jax.random.randint(streams_of[4], (N_DP, IMAX), 0, NCLS), jax.random.fold_in(streams_of[4], 1), 0, NCLS - 1).astype(jnp.int32)
    class_table = scatter_about(streams_of[5], (NCLS, D), 1.0, 6.0, ((1, 4),))
    w_ada = scatter_about(streams_of[6], (LAYERS, D, 6 * D), D ** -0.5, 0.1875, ((1, 4), (2, 8)))
    w_qkv = scatter_about(streams_of[7], (LAYERS, D, 3, D), D ** -0.5, 0.1875, ((1, 8), (3, 4)))
    head_scale = jnp.clip(2.1 + 1.1000001 * jax.random.uniform(streams_of[8], (LAYERS, HEADS), jnp.float32) ** level_of(streams_of[8], (LAYERS, HEADS), ((1, 4),), -0.2, 0.2), 2.1, 3.2)
    w_proj = scatter_about(streams_of[9], (LAYERS, D, D), (D // 8) ** -0.5, 0.5, ((1, 4), (2, 8)))
    w_fc1 = scatter_about(streams_of[10], (LAYERS, D, FF), D ** -0.5, 0.1875, ((1, 8), (2, 4)))
    w_fc2 = scatter_about(streams_of[11], (LAYERS, FF, D), FF ** -0.5, 0.09375, ((1, 4), (2, 8)))
    return dict(tokens=tokens, out_grad=out_grad, dest=dest, lengths=lengths, classes=classes, class_table=class_table, w_ada=w_ada, w_qkv=w_qkv, head_scale=head_scale, w_proj=w_proj, w_fc1=w_fc1, w_fc2=w_fc2)


highest = lax.Precision.HIGHEST
epsilon = 1e-06
masked_score = -1e+30
level_ends = (1, 5, 14, 30, 55, 91, 155, 255, 424, 680)

@jax.custom_vjp
def low(v):
    return lax.optimization_barrier(v.astype(jnp.bfloat16)).astype(jnp.float32)

@jax.custom_vjp
def low_back(v):
    return v

def low_keep(v):
    return (low(v), None)

def low_pass(kept, grad):
    return (grad,)

def back_keep(v):
    return (v, None)

def back_low(kept, grad):
    return (low(grad),)
low.defvjp(low_keep, low_pass)
low_back.defvjp(back_keep, back_low)

def layer_norm(value):
    centered = value - lax.optimization_barrier(jnp.mean(value, axis=-1, keepdims=True))
    return centered * lax.rsqrt(lax.optimization_barrier(jnp.mean(centered * centered, axis=-1, keepdims=True)) + epsilon)

def unit_rows(value):
    return value * lax.rsqrt(lax.optimization_barrier(jnp.sum(value * value, axis=-1, keepdims=True)) + epsilon)

def pack_layout(lengths, rows):
    ends = jnp.cumsum(lengths.astype(jnp.int32)).astype(jnp.int32)
    starts = (ends - lengths.astype(jnp.int32)).astype(jnp.int32)
    place = jnp.arange(rows, dtype=jnp.int32)
    member = lax.optimization_barrier(jnp.sum((place[:, None] >= ends[None, :]).astype(jnp.int32), axis=1)).astype(jnp.int32)
    onehot = member[:, None] == jnp.arange(lengths.shape[0], dtype=jnp.int32)[None, :]
    start = lax.optimization_barrier(jnp.sum(jnp.where(onehot, starts[None, :], jnp.int32(0)), axis=1)).astype(jnp.int32)
    bounds = jnp.array(level_ends, dtype=jnp.int32)
    level = lax.optimization_barrier(jnp.sum(((place - start)[:, None] >= bounds[None, :]).astype(jnp.int32), axis=1)).astype(jnp.int32)
    allowed = (member[:, None] == member[None, :]) & (level[None, :] <= level[:, None])
    return (onehot, allowed)

def pack_forward(carried, onehot, allowed, cond, weights):
    w_ada, w_qkv, head_scale, w_proj, w_fc1, w_fc2 = weights
    rows, width = carried.shape
    heads = head_scale.shape[1]
    spread = onehot.astype(carried.dtype)
    cond_low = low(jax.nn.silu(cond))
    for layer in range(w_ada.shape[0]):
        modulation = low_back(jnp.dot(cond_low, w_ada[layer], precision=highest))
        per_token = jnp.dot(spread, modulation, precision=highest)
        gain_one = per_token[:, 0:width]
        gain_two = per_token[:, width:2 * width]
        scale_one = per_token[:, 2 * width:3 * width]
        scale_two = per_token[:, 3 * width:4 * width]
        shift_one = per_token[:, 4 * width:5 * width]
        shift_two = per_token[:, 5 * width:6 * width]
        first_input = low(layer_norm(carried) * (1.0 + scale_one) + shift_one)
        projected = low_back(jnp.einsum('td,dcf->tcf', first_input, w_qkv[layer], precision=highest))
        query = projected[:, 0].reshape(rows, heads, -1)
        key_part = projected[:, 1].reshape(rows, heads, -1)
        values = low(projected[:, 2].reshape(rows, heads, -1))
        queries = low(unit_rows(query) * jnp.exp(head_scale[layer])[None, :, None])
        keys = low(unit_rows(key_part))
        scores = low_back(jnp.einsum('thd,shd->hts', queries, keys, precision=highest))
        probs = jax.nn.softmax(jnp.where(allowed[None], scores, masked_score), axis=-1)
        heads_out = low(low_back(jnp.einsum('hts,shd->thd', low(probs), values, precision=highest))).reshape(rows, width)
        attended = low_back(jnp.dot(heads_out, w_proj[layer], precision=highest))
        middle = carried + gain_one * attended
        second_input = low(layer_norm(middle) * (1.0 + scale_two) + shift_two)
        hidden = low_back(jnp.dot(second_input, w_fc1[layer], precision=highest))
        activated = low(jax.nn.gelu(hidden, approximate=True))
        branch = low_back(jnp.dot(activated, w_fc2[layer], precision=highest))
        carried = middle + gain_two * branch
    return carried

def reference(tokens, out_grad, dest, lengths, classes, class_table, w_ada, w_qkv, head_scale, w_proj, w_fc1, w_fc2):
    groups, shards, rows = dest.shape
    pack = shards * rows
    width = tokens.shape[1]
    places = jnp.arange(groups * shards * rows, dtype=jnp.int32)
    shard_ids = jnp.arange(shards, dtype=jnp.int32)[None, :, None]
    targets = ((dest // rows * shards + shard_ids) * rows + dest % rows).reshape(-1).astype(jnp.int32)
    sources = jnp.zeros(groups * shards * rows, jnp.int32).at[targets].set(places)

    def forward(flat_tokens, table, ada, qkv, scale, proj, fc1, fc2):
        packed = flat_tokens[sources].reshape(groups, pack, width)

        def one_pack(carry, inputs):
            pack_tokens, pack_lengths, pack_classes = inputs
            onehot, allowed = pack_layout(pack_lengths, pack)
            result = pack_forward(pack_tokens, onehot, allowed, table[pack_classes], (ada, qkv, scale, proj, fc1, fc2))
            return (carry, result)
        _, outputs = lax.scan(jax.checkpoint(one_pack), jnp.zeros((), jnp.int32), (packed, lengths, classes))
        return outputs.reshape(-1, width)[targets]
    floats = (tokens.astype(jnp.float32), class_table.astype(jnp.float32), w_ada.astype(jnp.float32), w_qkv.astype(jnp.float32), head_scale.astype(jnp.float32), w_proj.astype(jnp.float32), w_fc1.astype(jnp.float32), w_fc2.astype(jnp.float32))
    mixed, pull = jax.vjp(forward, *floats)
    grads = pull(out_grad.astype(jnp.float32))
    return (mixed.astype(jnp.bfloat16), grads[0].astype(jnp.bfloat16), grads[1], grads[2], grads[3], grads[4], grads[5], grads[6], grads[7])
```

```python
import jax
import jax.numpy as jnp
from jax import lax
from jax.sharding import PartitionSpec as P

epsilon = 1e-06
masked_score = -1e30
level_ends = (1, 5, 14, 30, 55, 91, 155, 255, 424, 680)
wide = jnp.float32
low = jnp.bfloat16


def matmul(left, right):
    return jnp.dot(left, right, preferred_element_type=wide)


def contract_rows(left, right):
    return lax.dot_general(left, right, (((0,), (0,)), ((), ())), preferred_element_type=wide)


def contract_last(left, right):
    return lax.dot_general(left, right, (((1,), (1,)), ((), ())), preferred_element_type=wide)


def layer_norm(value):
    centered = value - jnp.mean(value, axis=-1, keepdims=True)
    return centered * lax.rsqrt(jnp.mean(centered * centered, axis=-1, keepdims=True) + epsilon)


def modulate(value, scale, shift):
    return layer_norm(value) * (1.0 + scale) + shift


def unit_rows(value):
    return value * lax.rsqrt(jnp.sum(value * value, axis=-1, keepdims=True) + epsilon)


def query_norm(value, log_scale):
    return unit_rows(value) * jnp.exp(log_scale)[None, :, None]


def gelu_tanh(value):
    return jax.nn.gelu(value, approximate=True)


def swap(value, axis, offset):
    size = lax.axis_size(axis)
    return lax.ppermute(value, axis, [(i, i ^ offset) for i in range(size)])


def after(value, marker):
    return lax.optimization_barrier((value, marker))[0]


def paired(groups):
    return groups == 8


def block_order(groups):
    half = [offset for offset in range(groups) if offset % 2 == 0]
    return half + [offset + 1 for offset in half]


def to_own_order(value, axis, groups):
    if not paired(groups):
        return value
    here = lax.axis_index("dp")
    width = value.shape[axis]
    lead, tail = value.shape[:axis], value.shape[axis + 1 :]
    split = value.reshape(lead + (2, 2, 2, width // 8) + tail)
    return split, here


def into_order(value, groups):
    if not paired(groups):
        return value
    here = lax.axis_index("dp")
    shape = value.shape
    width = shape[-1] // groups
    blocks = value.reshape(shape[:-1] + (groups, width))
    ordered = [
        lax.dynamic_index_in_dim(blocks, here ^ offset, blocks.ndim - 2, keepdims=False)
        for offset in block_order(groups)
    ]
    return jnp.concatenate(ordered, axis=-1)


def from_order(value, groups):
    if not paired(groups):
        return value
    here = lax.axis_index("dp")
    shape = value.shape
    width = shape[-1] // groups
    blocks = value.reshape(shape[:-1] + (groups, width))
    order = block_order(groups)
    place = jnp.array([order.index(offset) for offset in range(groups)], jnp.int32)
    ordered = [
        lax.dynamic_index_in_dim(blocks, place[here ^ index], blocks.ndim - 2, keepdims=False)
        for index in range(groups)
    ]
    return jnp.concatenate(ordered, axis=-1)


def gather_blocks(block, axis):
    groups = lax.axis_size("dp")
    if not paired(groups):
        return lax.all_gather(block, "dp", axis=axis, tiled=True)
    held = [block] + [swap(block, "dp", offset) for offset in (2, 4, 6)]
    held = held + [swap(part, "dp", 1) for part in held]
    return jnp.concatenate(held, axis=axis)


def scatter_sum(kept, sent, axis):
    groups = lax.axis_size("dp")
    if not paired(groups):
        whole = jnp.concatenate([kept.astype(low), sent.astype(low)], axis=axis)
        return lax.psum_scatter(whole, "dp", scatter_dimension=axis, tiled=True).astype(wide)
    total = kept + swap(sent.astype(low), "dp", 1).astype(wide)
    span = total.shape[axis] // 4
    parts = [lax.slice_in_dim(total, i * span, (i + 1) * span, axis=axis) for i in range(4)]
    arrived = [swap(parts[i].astype(low), "dp", 2 * i).astype(wide) for i in (1, 2, 3)]
    return parts[0] + arrived[0] + arrived[1] + arrived[2]


def widen(value):
    return jnp.concatenate([value, swap(value, "shard", 1)], axis=0)


def narrow(value):
    half = value.shape[0] // 2
    here = (value[:half] + swap(value[half:].astype(low), "shard", 1).astype(wide)).astype(low)
    there = swap(here, "shard", 2)
    quarter = half // 2
    there = jnp.concatenate([there[quarter:], there[:quarter]], axis=0)
    return here.astype(wide) + there.astype(wide)


def route(dest, rows):
    table = dest[:, 0, :]
    groups = table.shape[0]
    capacity = rows // groups
    here = lax.axis_index("dp")
    own = lax.dynamic_index_in_dim(table, here, 0, keepdims=False)
    pack = own // rows
    index = jnp.arange(rows, dtype=jnp.int32)
    earlier = index[None, :] < index[:, None]
    rank = jnp.sum((earlier & (pack[None, :] == pack[:, None])).astype(jnp.int32), axis=1)
    slot = pack * capacity + rank
    to_slots = (slot[None, :] == index[:, None]).astype(low)
    mine = table // rows == here
    rank_in = jnp.sum((earlier[None] & mine[:, None, :]).astype(jnp.int32), axis=2)
    slot_in = jnp.arange(groups, dtype=jnp.int32)[:, None] * capacity + rank_in
    slot_in = jnp.where(mine, slot_in, rows).reshape(-1)
    row_in = (table % rows).reshape(-1)
    by_row = (row_in[None, :] == index[:, None]).astype(low)
    by_slot = (slot_in[None, :] == index[:, None]).astype(low)
    to_rows = contract_last(by_row, by_slot).astype(low)
    return to_slots, to_rows


def exchange(value, groups):
    return lax.all_to_all(value, "dp", split_axis=0, concat_axis=0, tiled=True)


def pack_layout(lengths, place):
    ends = jnp.cumsum(lengths)
    starts = ends - lengths
    member = jnp.sum((place[:, None] >= ends[None, :]).astype(jnp.int32), axis=1)
    onehot = member[:, None] == jnp.arange(lengths.shape[0], dtype=jnp.int32)[None, :]
    start = jnp.sum(jnp.where(onehot, starts[None, :], jnp.int32(0)), axis=1)
    bounds = jnp.array(level_ends, dtype=jnp.int32)
    level = jnp.sum(((place - start)[:, None] >= bounds[None, :]).astype(jnp.int32), axis=1)
    allowed = (member[:, None] == member[None, :]) & (level[None, :] <= level[:, None])
    return member, allowed


def attend(queries, keys, values, allowed):
    scores = jnp.einsum("thd,shd->hts", queries, keys, preferred_element_type=wide)
    scores = jnp.where(allowed[None], scores, masked_score)
    top = jnp.max(scores, axis=-1, keepdims=True)
    raised = jnp.exp(scores - top)
    total = jnp.sum(raised, axis=-1, keepdims=True)
    probs = (raised / total).astype(low)
    outputs = jnp.einsum("hts,shd->thd", probs, values, preferred_element_type=wide)
    return outputs, top + jnp.log(total)


def attend_back(queries, keys, values, allowed, log_total, grad_heads):
    scores = jnp.einsum("thd,shd->hts", queries, keys, preferred_element_type=wide)
    probs = jnp.where(allowed[None], jnp.exp(scores - log_total), 0.0)
    grad_probs = jnp.einsum("thd,shd->hts", grad_heads, values, preferred_element_type=wide)
    inner = jnp.sum(probs * grad_probs, axis=-1, keepdims=True)
    grad_scores = (probs * (grad_probs - inner)).astype(low)
    grad_queries = jnp.einsum("hts,shd->thd", grad_scores, keys, preferred_element_type=wide)
    grad_keys = jnp.einsum("hts,thd->shd", grad_scores, queries, preferred_element_type=wide)
    grad_values = jnp.einsum("hts,thd->shd", probs.astype(low), grad_heads, preferred_element_type=wide)
    return grad_queries, grad_keys, grad_values


def on_device(
    tokens,
    out_grad,
    dest,
    lengths,
    classes,
    class_table,
    w_ada,
    w_qkv,
    head_scale,
    w_proj,
    w_fc1,
    w_fc2,
):
    rows, width = tokens.shape
    groups, shards = lax.axis_size("dp"), lax.axis_size("shard")
    layers = w_ada.shape[0]
    pack = rows * shards
    heads_here = head_scale.shape[1]
    items = lengths.shape[1]
    slots = rows // groups
    columns = w_ada.shape[2]
    me = lax.axis_index("shard")

    to_slots, to_rows = route(dest, rows)
    coded = jnp.concatenate([classes[0] // 32, classes[0] % 32]).astype(low)
    coded = jnp.pad(coded, (0, width - 2 * items))
    leaving = jnp.concatenate(
        [
            matmul(to_slots, tokens).astype(low).reshape(groups, slots, width),
            jnp.broadcast_to(coded[None, None], (groups, 1, width)),
        ],
        axis=1,
    )
    arrived = exchange(leaving, groups)
    packed = matmul(to_rows, arrived[:, :slots].reshape(rows, width)).astype(low)
    packed = into_order(packed, groups)
    carried = jnp.concatenate([packed, swap(packed, "shard", 2)], axis=0).astype(wide)
    codes = arrived[:, slots, : 2 * items].astype(jnp.int32)
    all_classes = (codes[:, :items] * 32 + codes[:, items:]).reshape(-1)

    hits = (all_classes[:, None] == jnp.arange(class_table.shape[0], dtype=jnp.int32)[None, :]).astype(low)
    cond = matmul(hits, class_table)
    cond_low = jax.nn.silu(cond).astype(low)
    part = jnp.stack([matmul(cond_low, w_ada[layer]) for layer in range(layers)])
    part = part + swap(part, "shard", 1)
    part = part + swap(part, "shard", 2)
    part = jnp.swapaxes(part.reshape(layers, groups, items, columns), 0, 1)
    upper = lax.reduce_precision(part, 8, 7)
    both = jnp.stack([upper.astype(low), (part - upper).astype(low)], axis=1)
    both = both.reshape(groups, -1, width if (2 * layers * items * columns) % width == 0 else columns)
    grads_out = matmul(to_slots, out_grad).astype(low).reshape(groups, slots, width)
    if both.shape[2] == width:
        lines = both.shape[1]
        mixed_in = exchange(jnp.concatenate([both, grads_out], axis=1), groups)
        both, grads_out = mixed_in[:, :lines], mixed_in[:, lines:]
    else:
        both, grads_out = exchange(both, groups), exchange(grads_out, groups)
    both = both.reshape(groups, 2, layers, items, columns).astype(wide)
    modulation = jnp.transpose(both[:, 0] + both[:, 1], (1, 2, 0, 3)).reshape(layers, items, 6, width)
    modulation = into_order(modulation, groups)
    grad_packed = matmul(to_rows, grads_out.reshape(rows, width)).astype(low)
    grad_packed = into_order(grad_packed, groups)
    grad_carried = jnp.concatenate([grad_packed, swap(grad_packed, "shard", 2)], axis=0).astype(wide)

    place = jnp.concatenate(
        [(me ^ offset) * rows + jnp.arange(rows, dtype=jnp.int32) for offset in (0, 2, 1, 3)]
    )
    member, allowed = pack_layout(lengths[0], place)
    member_here = member[: 2 * rows, None]

    def spread(layer, part):
        choice = modulation[layer, :, part]
        result = choice[items - 1][None]
        for item in range(items - 2, -1, -1):
            result = jnp.where(member_here == item, choice[item][None], result)
        return result

    gains = [(spread(l, 0), spread(l, 1)) for l in range(layers)]
    scales = [(spread(l, 2), spread(l, 3)) for l in range(layers)]
    shifts = [(spread(l, 4), spread(l, 5)) for l in range(layers)]

    weights = []
    for layer in range(layers):
        qkv = w_qkv[layer].reshape(w_qkv.shape[1], -1)
        weights.append(
            (
                gather_blocks(qkv, 0),
                gather_blocks(w_proj[layer], 1),
                gather_blocks(w_fc1[layer], 0),
                gather_blocks(w_fc2[layer], 1),
            )
        )

    saved = []
    for layer in range(layers):
        qkv_full, proj_full, fc1_full, fc2_full = weights[layer]
        gain_one, gain_two = gains[layer]
        scale_one, scale_two = scales[layer]
        shift_one, shift_two = shifts[layer]
        first_all = widen(modulate(carried, scale_one, shift_one).astype(low))
        projected = matmul(first_all, qkv_full)
        span = projected.shape[1] // 3
        query = projected[:, :span].reshape(pack, heads_here, -1)
        key_part = projected[:, span : 2 * span].reshape(pack, heads_here, -1)
        values = projected[:, 2 * span :].reshape(pack, heads_here, -1).astype(low)
        queries = query_norm(query, head_scale[layer]).astype(low)
        keys = unit_rows(key_part).astype(low)
        heads_out, log_total = attend(queries, keys, values, allowed)
        heads_low = heads_out.reshape(pack, -1).astype(low)
        attended = narrow(matmul(heads_low, proj_full))
        middle = carried + gain_one * attended
        second_all = widen(modulate(middle, scale_two, shift_two).astype(low))
        hidden = matmul(second_all, fc1_full)
        activated = gelu_tanh(hidden).astype(low)
        branch = narrow(matmul(activated, fc2_full))
        saved.append(
            (carried, middle, first_all, query, key_part, queries, keys, values, log_total)
            + (heads_low, attended, second_all, hidden, activated, branch)
        )
        carried = middle + gain_two * branch

    choose = (member_here == jnp.arange(items, dtype=jnp.int32)[None, :]).astype(wide)

    def item_sums(value):
        return lax.dot_general(
            choose, value, (((0,), (0,)), ((), ())), precision=lax.Precision.HIGHEST
        )

    mixed_out = matmul(to_rows.T, from_order(carried[:rows].astype(low), groups)).astype(low)
    mixed_out = mixed_out.reshape(groups, slots, width)

    layer_grads = [None] * layers
    scale_grads = [None] * layers
    mod_grads = [None] * layers
    for layer in range(layers - 1, -1, -1):
        qkv_full, proj_full, fc1_full, fc2_full = weights[layer]
        gain_one, gain_two = gains[layer]
        scale_one, scale_two = scales[layer]
        shift_one, shift_two = shifts[layer]
        (
            carried_in,
            middle,
            first_all,
            query,
            key_part,
            queries,
            keys,
            values,
            log_total,
            heads_low,
            attended,
            second_all,
            hidden,
            activated,
            branch,
        ) = saved[layer]
        half = width // 2
        grad_gain_two = grad_carried * branch
        grad_branch = widen((grad_carried * gain_two).astype(low))
        grad_activated = contract_last(grad_branch, fc2_full)
        _, gelu_pull = jax.vjp(gelu_tanh, hidden)
        grad_hidden = gelu_pull(grad_activated)[0].astype(low)
        grad_second = narrow(contract_last(grad_hidden, fc1_full))
        grad_fc2 = scatter_sum(
            contract_rows(activated, grad_branch[:, :half]), contract_rows(activated, grad_branch[:, half:]), 1
        )
        grad_fc1 = scatter_sum(
            contract_rows(second_all[:, :half], grad_hidden), contract_rows(second_all[:, half:], grad_hidden), 0
        )
        _, second_pull = jax.vjp(modulate, middle, scale_two, shift_two)
        grad_middle_part, grad_scale_two, grad_shift_two = second_pull(grad_second)
        grad_middle = grad_carried + grad_middle_part
        grad_gain_one = grad_middle * attended
        grad_attended = widen((grad_middle * gain_one).astype(low))
        grad_heads = contract_last(grad_attended, proj_full).astype(low).reshape(pack, heads_here, -1)
        grad_queries, grad_keys, grad_values = attend_back(
            queries, keys, values, allowed, log_total, grad_heads
        )
        _, query_pull = jax.vjp(query_norm, query, head_scale[layer])
        grad_query, grad_log = query_pull(grad_queries)
        _, key_pull = jax.vjp(unit_rows, key_part)
        (grad_key,) = key_pull(grad_keys)
        grad_projected = jnp.concatenate(
            [grad_query.reshape(pack, -1), grad_key.reshape(pack, -1), grad_values.reshape(pack, -1)], axis=1
        ).astype(low)
        grad_first = narrow(contract_last(grad_projected, qkv_full))
        grad_proj = scatter_sum(
            contract_rows(heads_low, grad_attended[:, :half]), contract_rows(heads_low, grad_attended[:, half:]), 1
        )
        grad_qkv = scatter_sum(
            contract_rows(first_all[:, :half], grad_projected), contract_rows(first_all[:, half:], grad_projected), 0
        )
        _, first_pull = jax.vjp(modulate, carried_in, scale_one, shift_one)
        grad_carried_part, grad_scale_one, grad_shift_one = first_pull(grad_first)
        grad_carried = grad_middle + grad_carried_part
        sums = jnp.stack(
            [
                item_sums(term)
                for term in (
                    grad_gain_one,
                    grad_gain_two,
                    grad_scale_one,
                    grad_scale_two,
                    grad_shift_one,
                    grad_shift_two,
                )
            ],
            axis=1,
        )
        sums = (sums + swap(sums, "shard", 1)).astype(low)
        mod_grads[layer] = from_order(sums, groups).reshape(items, groups, columns)
        scale_grads[layer] = grad_log
        layer_grads[layer] = (grad_qkv.reshape(w_qkv.shape[1:]), grad_proj, grad_fc1, grad_fc2)

    grads_back = matmul(to_rows.T, from_order(grad_carried[:rows].astype(low), groups)).astype(low)
    grads_back = grads_back.reshape(groups, slots, width)
    sent = jnp.swapaxes(jnp.stack(mod_grads), 0, 2).reshape(groups, items * layers * columns)
    if sent.shape[1] % width:
        mods_back = exchange(sent, groups)
        rows_back = exchange(jnp.concatenate([mixed_out, grads_back], axis=1), groups)
    else:
        sent = sent.reshape(groups, -1, width)
        back = exchange(jnp.concatenate([mixed_out, grads_back, sent], axis=1), groups)
        rows_back, mods_back = back[:, : 2 * slots], back[:, 2 * slots :]
    mixed = matmul(to_slots.T, rows_back[:, :slots].reshape(rows, width)).astype(low)
    tokens_grad = matmul(to_slots.T, rows_back[:, slots:].reshape(rows, width)).astype(low)
    mods_back = mods_back.reshape(groups, items, layers, columns)
    mods_back = jnp.swapaxes(mods_back, 1, 2)
    grad_silu = jnp.zeros(cond.shape, wide)
    ada_grads = []
    for layer in range(layers):
        grad_modulation = mods_back[:, layer].reshape(groups * items, columns)
        ada_grads.append(contract_rows(cond_low, grad_modulation))
        grad_silu = grad_silu + contract_last(grad_modulation, w_ada[layer])
    logs = jnp.pad(jnp.stack(scale_grads).reshape(1, -1), ((0, 7), (0, cond.shape[1] - layers * heads_here)))
    summed = jnp.concatenate([grad_silu, logs], axis=0)
    if paired(groups):
        for offset in (1, 2, 4):
            summed = summed + swap(summed, "dp", offset)
    else:
        summed = lax.psum(summed, "dp")
    grad_silu = summed[: cond.shape[0]]
    scale_grad = summed[cond.shape[0], : layers * heads_here].reshape(layers, heads_here)
    _, silu_pull = jax.vjp(jax.nn.silu, cond)
    (grad_cond,) = silu_pull(grad_silu)
    table_grad = lax.dot_general(
        hits.astype(wide), grad_cond, (((0,), (0,)), ((), ())), precision=lax.Precision.HIGHEST
    )
    qkv_grad, proj_grad, fc1_grad, fc2_grad = (
        jnp.stack([layer_grads[layer][i] for layer in range(layers)]) for i in range(4)
    )
    return (
        mixed,
        tokens_grad,
        table_grad,
        jnp.stack(ada_grads),
        qkv_grad,
        scale_grad,
        proj_grad,
        fc1_grad,
        fc2_grad,
    )


def solution(mesh):
    placed = (
        P(("dp", "shard"), None),
        P(("dp", "shard"), None),
        P(None, "shard", None),
        P("dp", None),
        P("dp", None),
        P(None, "shard"),
        P(None, "shard", "dp"),
        P(None, "dp", None, "shard"),
        P(None, "shard"),
        P(None, "shard", "dp"),
        P(None, "dp", "shard"),
        P(None, "shard", "dp"),
    )
    return jax.shard_map(
        on_device,
        mesh=mesh,
        in_specs=placed,
        out_specs=(
            P(("dp", "shard"), None),
            P(("dp", "shard"), None),
            P(None, "shard"),
            P(None, "shard", "dp"),
            P(None, "dp", None, "shard"),
            P(None, "shard"),
            P(None, "shard", "dp"),
            P(None, "dp", "shard"),
            P(None, "shard", "dp"),
        ),
        check_vma=False,
    )
```

```python
import functools

import jax
import jax.numpy as jnp
from jax import lax
from jax.experimental import pallas as pl
from jax.experimental.pallas import tpu as pltpu
from jax.sharding import PartitionSpec as P

epsilon = 1e-06
level_ends = (1, 5, 14, 30, 55, 91, 155, 255, 424, 680)
wide = jnp.float32
low = jnp.bfloat16
root = 0.7978845608028654
cubic = 0.044715


def matmul(left, right):
    return jnp.dot(left, right, preferred_element_type=wide)


def contract_rows(left, right):
    return lax.dot_general(left, right, (((0,), (0,)), ((), ())), preferred_element_type=wide)


def contract_last(left, right):
    return lax.dot_general(left, right, (((1,), (1,)), ((), ())), preferred_element_type=wide)


def swap(value, axis, offset):
    size = lax.axis_size(axis)
    return lax.ppermute(value, axis, [(i, i ^ offset) for i in range(size)])


def tie(value, *others):
    return lax.optimization_barrier((value, others))[0]


slow_groups = [[0, 2, 4, 6], [1, 3, 5, 7]]


def paired(groups):
    return groups == 8


def own_order(groups):
    here = lax.axis_index("dp")
    if not paired(groups):
        return jnp.arange(groups, dtype=jnp.int32)
    place = jnp.arange(groups, dtype=jnp.int32)
    return (lax.rem(here // 2 + 4 - place % 4, 4) * 2 + (here % 2 ^ place // 4)).astype(jnp.int32)


def straight(block):
    return [lax.ppermute(block, "dp", [(i, (i + 2 * back) % 8) for i in range(8)]) for back in (1, 2, 3)]


def columns_of(piece, out, first):
    depth, width = piece.shape
    for index in range(width // 128):
        out[first + index * depth : first + (index + 1) * depth, :] = piece[:, index * 128 : (index + 1) * 128]


def pack_mix_kernel(qkv, proj, *refs, layer):
    out = refs[-1]
    columns_of(qkv[...], out, 0)
    first = qkv.shape[0] * qkv.shape[1] // 128
    out[first : first + proj.shape[1], :] = proj[layer]
    if len(refs) > 1:
        out[first + proj.shape[1] :, :] = refs[0][layer]


def pack_mix(qkv, proj, layer, *more):
    height = qkv.shape[0] * qkv.shape[1] // 128 + proj.shape[1] + sum(value.shape[1] for value in more)
    return call(functools.partial(pack_mix_kernel, layer=layer), [((height, 128), low)], qkv, proj, *more)[0]


def pack_fc1_kernel(fc1, out, *, layer):
    columns_of(fc1[layer], out, 0)


def pack_fc1(fc1, layer):
    height = fc1.shape[1] * fc1.shape[2] // 128
    return call(functools.partial(pack_fc1_kernel, layer=layer), [((height, 128), low)], fc1)[0]


def stack_kernel(*refs):
    out = refs[-1]
    size = refs[0].shape[0]
    for index, ref in enumerate(refs[:-1]):
        out[index * size : (index + 1) * size, :] = ref[...]


def stack(blocks):
    size = blocks[0].shape[0]
    return call(stack_kernel, [((size * len(blocks), 128), low)], *blocks)[0]


def put_block(read, place, outs, parts):
    first = 0
    for out, (depth, columns, axis) in zip(outs, parts):
        for index in range(columns):
            piece = read(first, depth)
            first += depth
            if axis == 0:
                out[place * depth : (place + 1) * depth, index * 128 : (index + 1) * 128] = piece
            else:
                out[:, place * 128 : (place + 1) * 128] = piece


def join_kernel(*refs, sources, parts):
    outs = refs[-len(parts) :]
    for place, (ref, base) in enumerate(sources):
        put_block(lambda first, depth: refs[ref][base + first : base + first + depth, :], place, outs, parts)


def pair_kernel(order, here, there, *outs, parts):
    size = here.shape[0] // 4
    for place in range(8):
        base = (order[place] // 2) * size
        blocks = there if place // 4 else here
        put_block(
            lambda first, depth: blocks[pl.ds(pl.multiple_of(base + first, 128), depth), :], place, outs, parts
        )


def join_pair(here, there, order, parts):
    return call(functools.partial(pair_kernel, parts=parts), joined_shapes(8, parts), order, here, there, scalars=1)


def order_kernel(order, blocks, *outs, parts):
    size = blocks.shape[0] // order.shape[0]
    for place in range(order.shape[0]):
        base = order[place] * size
        put_block(
            lambda first, depth: blocks[pl.ds(pl.multiple_of(base + first, 128), depth), :], place, outs, parts
        )


def joined_shapes(count, parts):
    return [((depth, 128 * count) if axis else (depth * count, columns * 128), low) for depth, columns, axis in parts]


def join(arrays, sources, parts):
    return call(
        functools.partial(join_kernel, sources=sources, parts=parts), joined_shapes(len(sources), parts), *arrays
    )


def join_ordered(blocks, order, parts):
    return call(
        functools.partial(order_kernel, parts=parts), joined_shapes(order.shape[0], parts), order, blocks, scalars=1
    )


def unpack_kernel(order, to_rows, arrived, out, kept):
    kept[...] = matmul(to_rows[...], arrived[...]).astype(low)
    span = out.shape[1] // order.shape[0]
    for place in range(order.shape[0]):
        out[:, place * span : (place + 1) * span] = kept[:, pl.ds(pl.multiple_of(order[place] * span, span), span)]


def unpack(to_rows, arrived, order):
    if not paired(order.shape[0]):
        return matmul(to_rows, arrived).astype(low)
    shape = (to_rows.shape[0], arrived.shape[1])
    return call(
        unpack_kernel, [(shape, low)], order, to_rows, arrived, scratch=[pltpu.VMEM(shape, low)], scalars=1
    )[0]


def repack_kernel(order, to_rows, value, out, kept):
    rows, span = out.shape[0], out.shape[1] // order.shape[0]
    for place in range(order.shape[0]):
        at = pl.ds(pl.multiple_of(order[place] * span, span), span)
        kept[:, at] = value[:rows, place * span : (place + 1) * span].astype(low)
    out[...] = contract_rows(to_rows[...], kept[...]).astype(low)


def repack(to_rows, value, order):
    shape = (to_rows.shape[0], value.shape[1])
    if not paired(order.shape[0]):
        return matmul(to_rows.T, value[: shape[0]].astype(low)).astype(low)
    return call(
        repack_kernel, [(shape, low)], order, to_rows, value, scratch=[pltpu.VMEM(shape, low)], scalars=1
    )[0]


def collect_kernel(*refs, offsets):
    out = refs[-1]
    lines, width = out.shape[0], out.shape[1] // 6
    for part, (ref, first) in enumerate(zip(refs[:-1], offsets)):
        out[:, part * width : (part + 1) * width] = ref[:lines, first : first + width]


def collect(parts, width):
    return call(
        functools.partial(collect_kernel, offsets=[first for _, first in parts]),
        [((8, 6 * width), wide)],
        *[value for value, _ in parts],
    )[0]


def unspread_kernel(order, own, other, out):
    count, _, columns = out.shape
    blocks = columns // 128
    for part in range(6):
        for place in range(count):
            first = (part * count + place) * 128
            block = order[place] + part * count
            at = pl.ds(pl.multiple_of(lax.rem(block, blocks) * 128, 128), 128)
            out[block // blocks, :, at] = (own[:, first : first + 128] + other[:, first : first + 128]).astype(low)


def unspread(own, other, order, items, columns):
    count = order.shape[0]
    if paired(count):
        return call(unspread_kernel, [((count, own.shape[0], columns), low)], order, own, other, scalars=1)[0][:, :items]
    return jnp.swapaxes((own + other).astype(low)[:items].reshape(items, count, columns), 0, 1)


def spread_kernel(order, arrived, out):
    count, lines, columns = arrived.shape
    layers, parts, items, _ = out.shape
    blocks = columns // 128
    for part in range(parts):
        for place in range(count):
            block = order[place] + part * count
            source = block // blocks
            at = pl.ds(pl.multiple_of(lax.rem(block, blocks) * 128, 128), 128)
            rows = arrived[source, :, at].astype(wide)
            total = rows[: lines // 2] + rows[lines // 2 :]
            for layer in range(layers):
                out[layer, part, :, place * 128 : (place + 1) * 128] = total[layer * items : (layer + 1) * items]


def spread(arrived, order, layers, items, width):
    count, lines, columns = arrived.shape
    if paired(count):
        return call(spread_kernel, [((layers, 6, items, width), wide)], order, arrived, scalars=1)[0]
    halves = arrived.astype(wide).reshape(count, 2, layers, items, columns)
    whole = jnp.transpose(halves[:, 0] + halves[:, 1], (1, 2, 0, 3)).reshape(layers, items, 6, width)
    return jnp.swapaxes(whole, 1, 2)


def fold_kernel(slow, kept, arrived, out):
    span = out.shape[2]
    for back in range(4):
        columns = slice(back * span, (back + 1) * span)
        out[lax.rem(slow[0] + 4 - back, 4)] = (kept[:, columns] + arrived[:, columns].astype(wide)).astype(low)


def fold(kept, arrived, slow):
    height, half = kept.shape
    return call(fold_kernel, [((4, height, half // 4), low)], slow, kept, arrived, scalars=1)[0]


class Sums:
    def __init__(self, kept, sent):
        self.kept = kept
        self.arrived = swap(sent, "dp", 1)

    def fold(self, along, marker):
        if along:
            slow = (lax.axis_index("dp") // 2).astype(jnp.int32).reshape(1)
            blocks = fold(self.kept, tie(self.arrived, marker), slow)
            self.blocks = lax.psum_scatter(
                blocks, "dp", scatter_dimension=0, axis_index_groups=slow_groups, tiled=True
            )
            return
        self.blocks = None
        total = self.kept + tie(self.arrived, marker).astype(wide)
        span = total.shape[1] // 4
        self.parts = [total[:, i * span : (i + 1) * span] for i in range(4)]
        for back in (1, 2, 3):
            pairs = [(i, (i + 8 - 2 * back) % 8) for i in range(8)]
            self.parts[back] = lax.ppermute(self.parts[back].astype(low), "dp", pairs)

    def total(self, marker):
        if self.blocks is not None:
            return tie(self.blocks, marker).reshape(self.blocks.shape[1:]).astype(wide)
        parts = [tie(part, marker) for part in self.parts]
        return parts[0] + parts[1].astype(wide) + parts[2].astype(wide) + parts[3].astype(wide)


class WholeSums:
    def __init__(self, blocks):
        self.arrived = blocks
        self.result = lax.psum_scatter(blocks, "dp", scatter_dimension=0, tiled=True)

    def fold(self):
        pass

    def total(self, marker):
        return tie(self.result, marker).reshape(self.result.shape[1:]).astype(wide)


def gather_cores(part_own, part_other):
    return (part_own + swap(part_other, "shard", 1).astype(wide)).astype(low)


def route(dest, rows):
    table = dest[:, 0, :]
    groups = table.shape[0]
    capacity = rows // groups
    here = lax.axis_index("dp")
    own = lax.dynamic_index_in_dim(table, here, 0, keepdims=False)
    pack = own // rows
    index = jnp.arange(rows, dtype=jnp.int32)
    earlier = index[None, :] < index[:, None]
    rank = jnp.sum((earlier & (pack[None, :] == pack[:, None])).astype(jnp.int32), axis=1)
    slot = pack * capacity + rank
    to_slots = (slot[None, :] == index[:, None]).astype(low)
    mine = table // rows == here
    rank_in = jnp.sum((earlier[None] & mine[:, None, :]).astype(jnp.int32), axis=2)
    slot_in = jnp.arange(groups, dtype=jnp.int32)[:, None] * capacity + rank_in
    slot_in = jnp.where(mine, slot_in, rows).reshape(-1)
    row_in = (table % rows).reshape(-1)
    by_row = (row_in[None, :] == index[:, None]).astype(low)
    by_slot = (slot_in[None, :] == index[:, None]).astype(low)
    to_rows = contract_last(by_row, by_slot).astype(low)
    return to_slots, to_rows


def exchange(value, groups):
    return lax.all_to_all(value, "dp", split_axis=0, concat_axis=0, tiled=True)


def pack_layout(lengths, place):
    ends = jnp.cumsum(lengths)
    starts = ends - lengths
    member = jnp.sum((place[:, None] >= ends[None, :]).astype(jnp.int32), axis=1)
    onehot = member[:, None] == jnp.arange(lengths.shape[0], dtype=jnp.int32)[None, :]
    start = jnp.sum(jnp.where(onehot, starts[None, :], jnp.int32(0)), axis=1)
    bounds = jnp.array(level_ends, dtype=jnp.int32)
    level = jnp.sum(((place - start)[:, None] >= bounds[None, :]).astype(jnp.int32), axis=1)
    return member, level


grant = 24
small = pl.CostEstimate(flops=1000000000, bytes_accessed=1000000, transcendentals=0)
stripe = 64


def call(kernel, outs, *operands, scratch=(), scalars=0):
    spec = pl.BlockSpec(memory_space=pltpu.VMEM)
    return pl.pallas_call(
        kernel,
        out_shape=[jax.ShapeDtypeStruct(shape, kind) for shape, kind in outs],
        in_specs=[pl.BlockSpec(memory_space=pltpu.SMEM)] * scalars + [spec] * (len(operands) - scalars),
        out_specs=[spec] * len(outs),
        scratch_shapes=list(scratch),
        cost_estimate=small,
        compiler_params=pltpu.CompilerParams(vmem_limit_bytes=grant << 20),
    )(*operands)


def pick(member, table):
    items = table.shape[0]
    result = table[items - 1 : items, :]
    for item in range(items - 2, -1, -1):
        result = jnp.where(member == item, table[item : item + 1, :], result)
    return result


def normed(value):
    centered = value - jnp.mean(value, axis=-1, keepdims=True)
    inverse = lax.rsqrt(jnp.mean(centered * centered, axis=-1, keepdims=True) + epsilon)
    return centered * inverse, inverse


def stripes(rows, body):
    @pl.loop(0, rows // stripe)
    def _(index):
        first = pl.multiple_of(index * stripe, stripe)
        body(pl.ds(first, stripe), pl.ds(pl.multiple_of(lax.rem(first + rows // 2, rows), stripe), stripe))


def enter_kernel(value, mods, member, out, *, scale, shift):
    def body(at, _):
        who = member[at, :]
        unit, _inverse = normed(value[at, :])
        out[at, :] = (unit * (1.0 + pick(who, mods[scale])) + pick(who, mods[shift])).astype(low)

    stripes(value.shape[0], body)


def enter(value, mods, member, scale, shift):
    return call(
        functools.partial(enter_kernel, scale=scale, shift=shift), [(value.shape, low)], value, mods, member
    )[0]


def step_kernel(value, here, there, mods_gain, mods, member, out, low_out, *, gain, scale, shift):
    def body(at, across):
        who = member[at, :]
        branch = here[at, :].astype(wide) + there[across, :].astype(wide)
        total = value[at, :] + pick(who, mods_gain[gain]) * branch
        out[at, :] = total
        unit, _inverse = normed(total)
        low_out[at, :] = (unit * (1.0 + pick(who, mods[scale])) + pick(who, mods[shift])).astype(low)

    stripes(value.shape[0], body)


def step(value, here, there, mods_gain, mods, member, gain, scale, shift):
    return call(
        functools.partial(step_kernel, gain=gain, scale=scale, shift=shift),
        [(value.shape, wide), (value.shape, low)],
        value, here, there, mods_gain, mods, member,
    )


def leave_kernel(value, here, there, mods, member, out, *, gain):
    def body(at, across):
        branch = here[at, :].astype(wide) + there[across, :].astype(wide)
        out[at, :] = value[at, :] + pick(member[at, :], mods[gain]) * branch

    stripes(value.shape[0], body)


def leave(value, here, there, mods, member, gain):
    return call(
        functools.partial(leave_kernel, gain=gain), [(value.shape, wide)], value, here, there, mods, member
    )[0]


def mlp_kernel(own, other, fc1, fc2, part_own, part_other, hidden_out, act_out):
    half = own.shape[0]
    for place, source, target in ((0, own, part_own), (1, other, part_other)):
        @pl.loop(0, half // 128)
        def _(index):
            at = pl.ds(pl.multiple_of(index * 128, 128), 128)
            put = pl.ds(pl.multiple_of(place * half + index * 128, 128), 128)
            hidden = matmul(source[at, :], fc1[...])
            hidden_out[put, :] = hidden
            activated = (0.5 * hidden * (1.0 + jnp.tanh(root * (hidden + cubic * hidden * hidden * hidden)))).astype(low)
            act_out[put, :] = activated
            target[at, :] = matmul(activated, fc2[...]).astype(target.dtype)


def mlp(own, other, fc1, fc2):
    half, width = own.shape
    units = fc1.shape[1]
    return call(
        mlp_kernel,
        [((half, width), wide), ((half, width), low), ((2 * half, units), wide), ((2 * half, units), low)],
        own, other, fc1, fc2,
    )


def mlp_back_kernel(own, other, hidden_in, fc1, fc2, part_own, part_other, grad_out):
    half = own.shape[0]
    for place, source, target in ((0, own, part_own), (1, other, part_other)):
        @pl.loop(0, half // 128)
        def _(index):
            at = pl.ds(pl.multiple_of(index * 128, 128), 128)
            put = pl.ds(pl.multiple_of(place * half + index * 128, 128), 128)
            grad_activated = contract_last(source[at, :], fc2[...])
            hidden = hidden_in[put, :]
            square = hidden * hidden
            bent = jnp.tanh(root * (hidden + cubic * hidden * square))
            slope = 0.5 * (1.0 + bent) + 0.5 * hidden * (1.0 - bent * bent) * (root * (1.0 + 3.0 * cubic * square))
            grad_hidden = (grad_activated * slope).astype(low)
            grad_out[put, :] = grad_hidden
            target[at, :] = contract_last(grad_hidden, fc1[...]).astype(target.dtype)


def mlp_back(own, other, hidden, fc1, fc2):
    half, width = own.shape
    return call(
        mlp_back_kernel,
        [((half, width), wide), ((half, width), low), (hidden.shape, low)],
        own, other, hidden, fc1, fc2,
    )


def heads_of(shape, heads):
    lane = lax.broadcasted_iota(jnp.int32, shape, 1)
    span = shape[1] // heads
    return [(lane >= head * span) & (lane < (head + 1) * span) for head in range(heads)]


def head_sums(value, masks):
    return [jnp.sum(jnp.where(mask, value, 0.0), axis=1, keepdims=True) for mask in masks]


def by_head(columns, masks):
    result = columns[-1]
    for column, mask in zip(columns[-2::-1], masks[-2::-1]):
        result = jnp.where(mask, column, result)
    return result


def allowed_at(member, level, member_row, level_row, at):
    return (member[at, :] == member_row[...]) & (level_row[...] <= level[at, :])


def attend_kernel(
    own, other, qkv, proj, scale, member, level, member_row, level_row,
    part_own, part_other, raw_out, heads_out, inverse_out, queries, keys, values, *, heads,
):
    half = own.shape[0]
    span = qkv.shape[1] // 3
    block = 128
    for place, source in ((0, own), (1, other)):
        @pl.loop(0, half // block)
        def _(index):
            at = pl.ds(pl.multiple_of(index * block, block), block)
            put = pl.ds(pl.multiple_of(place * half + index * block, block), block)
            projected = matmul(source[at, :], qkv[...])
            raw_out[put, :] = projected
            masks = heads_of((block, span), heads)
            query, key = projected[:, :span], projected[:, span : 2 * span]
            query_sums, key_sums = head_sums(query * query, masks), head_sums(key * key, masks)
            query_scale = by_head(
                [lax.rsqrt(total + epsilon) * jnp.exp(scale[:, head : head + 1]) for head, total in enumerate(query_sums)], masks
            )
            key_scale = by_head([lax.rsqrt(total + epsilon) for total in key_sums], masks)
            queries[put, :] = (query * query_scale).astype(low)
            keys[put, :] = (key * key_scale).astype(low)
            values[put, :] = projected[:, 2 * span :].astype(low)

    rows = 2 * half
    for place, target in ((0, part_own), (1, part_other)):
        @pl.loop(0, half // block)
        def _(index):
            at = pl.ds(pl.multiple_of(index * block, block), block)
            put = pl.ds(pl.multiple_of(place * half + index * block, block), block)
            allowed = allowed_at(member, level, member_row, level_row, put)
            query = queries[put, :]
            masks = heads_of((block, span), heads)
            wide_masks = heads_of((rows, span), heads)
            outputs = jnp.zeros((block, span), wide)
            inverses = []
            for head in range(heads):
                scores = contract_last(jnp.where(masks[head], query, jnp.zeros_like(query)), keys[...])
                raised = jnp.where(allowed, jnp.exp(scores - jnp.exp(scale[:, head : head + 1])), 0.0)
                inverse = 1.0 / jnp.sum(raised, axis=1, keepdims=True)
                inverses.append(inverse)
                weights = (raised * inverse).astype(low)
                outputs = outputs + matmul(weights, jnp.where(wide_masks[head], values[...], jnp.zeros((), low)))
            inverse_out[put, :] = jnp.concatenate(inverses, axis=1)
            outputs = outputs.astype(low)
            heads_out[put, :] = outputs
            target[at, :] = matmul(outputs, proj[...]).astype(target.dtype)


def attend(own, other, qkv, proj, scale, layout, heads):
    half, width = own.shape
    rows, span = 2 * half, qkv.shape[1] // 3
    return call(
        functools.partial(attend_kernel, heads=heads),
        [
            ((half, width), wide),
            ((half, width), low),
            ((rows, 3 * span), wide),
            ((rows, span), low),
            ((rows, heads), wide),
        ],
        own, other, qkv, proj, scale, *layout,
        scratch=[pltpu.VMEM((rows, span), low)] * 3,
    )


def attend_back_kernel(
    own, other, raw, inverse_in, qkv, proj, scale, member, level, member_row, level_row,
    part_own, part_other, grad_out, log_out,
    queries, keys, values, grads, grad_queries, key_sums_t, value_sums_t, *, heads,
):
    half = own.shape[0]
    rows = 2 * half
    span = qkv.shape[1] // 3
    block = 128
    for place, source in ((0, own), (1, other)):
        @pl.loop(0, half // block)
        def _(index):
            at = pl.ds(pl.multiple_of(index * block, block), block)
            put = pl.ds(pl.multiple_of(place * half + index * block, block), block)
            grads[put, :] = contract_last(source[at, :], proj[...]).astype(low)
            masks = heads_of((block, span), heads)
            query, key = raw[put, :span], raw[put, span : 2 * span]
            query_sums, key_sums = head_sums(query * query, masks), head_sums(key * key, masks)
            query_scale = by_head(
                [lax.rsqrt(total + epsilon) * jnp.exp(scale[:, head : head + 1]) for head, total in enumerate(query_sums)], masks
            )
            key_scale = by_head([lax.rsqrt(total + epsilon) for total in key_sums], masks)
            queries[put, :] = (query * query_scale).astype(low)
            keys[put, :] = (key * key_scale).astype(low)
            values[put, :] = raw[put, 2 * span :].astype(low)

    key_sums_t[...] = jnp.zeros_like(key_sums_t)
    value_sums_t[...] = jnp.zeros_like(value_sums_t)
    deep = span // heads
    step_rows = 256

    @pl.loop(0, rows // step_rows)
    def _(index):
        put = pl.ds(pl.multiple_of(index * step_rows, step_rows), step_rows)
        allowed = allowed_at(member, level, member_row, level_row, put)
        query, grad = queries[put, :], grads[put, :]
        query_t, grad_t = query.astype(wide).T.astype(low), grad.astype(wide).T.astype(low)
        masks = heads_of((step_rows, span), heads)
        wide_masks = heads_of((rows, span), heads)
        outputs = jnp.zeros((step_rows, span), wide)
        for head in range(heads):
            scores = contract_last(jnp.where(masks[head], query, jnp.zeros_like(query)), keys[...])
            raised = jnp.where(allowed, jnp.exp(scores - jnp.exp(scale[:, head : head + 1])), 0.0)
            weights = raised * inverse_in[put, head : head + 1]
            grad_weights = contract_last(jnp.where(masks[head], grad, jnp.zeros_like(grad)), values[...])
            inner = jnp.sum(weights * grad_weights, axis=1, keepdims=True)
            grad_scores = (weights * (grad_weights - inner)).astype(low)
            outputs = outputs + matmul(grad_scores, jnp.where(wide_masks[head], keys[...], jnp.zeros((), low)))
            these = slice(head * deep, (head + 1) * deep)
            key_sums_t[these, :] += matmul(query_t[these, :], grad_scores)
            value_sums_t[these, :] += matmul(grad_t[these, :], weights.astype(low))
        grad_queries[put, :] = outputs

    log_out[...] = jnp.zeros_like(log_out)
    raw_keys = key_sums_t[...].T
    raw_values = value_sums_t[...].T
    grad_out[:, 2 * span :] = raw_values.astype(low)
    key_sums = raw_keys
    for place, target in ((0, part_own), (1, part_other)):
        for index in range(half // block):
            put = slice(place * half + index * block, place * half + (index + 1) * block)
            at = slice(index * block, (index + 1) * block)
            masks = heads_of((block, span), heads)
            query, key = raw[put, :span], raw[put, span : 2 * span]
            grad_query, grad_key = grad_queries[put, :], key_sums[put, :]
            inverse_q = [lax.rsqrt(total + epsilon) for total in head_sums(query * query, masks)]
            inverse_k = [lax.rsqrt(total + epsilon) for total in head_sums(key * key, masks)]
            dots_q, dots_k = head_sums(query * grad_query, masks), head_sums(key * grad_key, masks)
            rises = [jnp.exp(scale[:, head : head + 1]) for head in range(heads)]
            logs = [a * d * i for a, d, i in zip(rises, dots_q, inverse_q)]
            log_out[...] += jnp.concatenate([jnp.sum(x, axis=0, keepdims=True) for x in logs], axis=1)
            first = by_head([a * i for a, i in zip(rises, inverse_q)], masks)
            second = by_head([a * d * i * i * i for a, d, i in zip(rises, dots_q, inverse_q)], masks)
            grad_out[put, :span] = (grad_query * first - query * second).astype(low)
            first = by_head(inverse_k, masks)
            second = by_head([d * i * i * i for d, i in zip(dots_k, inverse_k)], masks)
            grad_out[put, span : 2 * span] = (grad_key * first - key * second).astype(low)
            target[at, :] = contract_last(grad_out[put, :], qkv[...]).astype(target.dtype)


def attend_back(own, other, raw, inverse, qkv, proj, scale, layout, heads):
    half, width = own.shape
    rows, span = 2 * half, qkv.shape[1] // 3
    return call(
        functools.partial(attend_back_kernel, heads=heads),
        [((half, width), wide), ((half, width), low), ((rows, 3 * span), low), ((1, heads), wide)],
        own, other, raw, inverse, qkv, proj, scale, *layout,
        scratch=[pltpu.VMEM((rows, span), low)] * 4
        + [pltpu.VMEM((rows, span), wide), pltpu.VMEM((span, rows), wide), pltpu.VMEM((span, rows), wide)],
    )


def step_back_kernel(
    value, here, there, grad, mods, mods_gain, branch_here, branch_there, member, choose,
    grad_out, low_out, sums_out, terms, *, scale, gain,
):
    width = value.shape[1]

    def body(at, across):
        who = member[at, :]
        unit, inverse = normed(value[at, :])
        arrived = here[at, :].astype(wide) + there[across, :].astype(wide)
        scaled = arrived * (1.0 + pick(who, mods[scale]))
        total = grad[at, :] + inverse * (
            scaled
            - jnp.mean(scaled, axis=-1, keepdims=True)
            - unit * jnp.mean(scaled * unit, axis=-1, keepdims=True)
        )
        grad_out[at, :] = total
        terms[at, : width] = (arrived * unit).astype(low)
        terms[at, width : 2 * width] = arrived.astype(low)
        if gain is not None:
            branch = branch_here[at, :].astype(wide) + branch_there[across, :].astype(wide)
            terms[at, 2 * width :] = (total * branch).astype(low)
            low_out[at, :] = (total * pick(who, mods_gain[gain])).astype(low)

    stripes(value.shape[0], body)
    sums_out[...] = matmul(choose[...], terms[...])


def last_back_kernel(value, here, there, grad, mods, member, choose, grad_out, sums_out, terms, *, scale):
    step_back_kernel(
        value, here, there, grad, mods, None, None, None, member, choose,
        grad_out, None, sums_out, terms, scale=scale, gain=None,
    )


def step_back(value, here, there, grad, mods, member, choose, scale, before=None):
    rows, width = value.shape
    lines = choose.shape[0]
    if before is None:
        return call(
            functools.partial(last_back_kernel, scale=scale),
            [((rows, width), wide), ((lines, 2 * width), wide)],
            value, here, there, grad, mods, member, choose,
            scratch=[pltpu.VMEM((rows, 2 * width), low)],
        )
    mods_gain, gain, branch_here, branch_there = before
    return call(
        functools.partial(step_back_kernel, scale=scale, gain=gain),
        [((rows, width), wide), ((rows, width), low), ((lines, 3 * width), wide)],
        value, here, there, grad, mods, mods_gain, branch_here, branch_there, member, choose,
        scratch=[pltpu.VMEM((rows, 3 * width), low)],
    )


def first_back_kernel(grad, here, there, mods, member, choose, low_out, sums_out, terms, *, gain):
    def body(at, across):
        branch = here[at, :].astype(wide) + there[across, :].astype(wide)
        terms[at, :] = (grad[at, :] * branch).astype(low)
        low_out[at, :] = (grad[at, :] * pick(member[at, :], mods[gain])).astype(low)

    stripes(grad.shape[0], body)
    sums_out[...] = matmul(choose[...], terms[...])


def first_back(grad, here, there, mods, member, choose, gain):
    rows, width = grad.shape
    return call(
        functools.partial(first_back_kernel, gain=gain),
        [((rows, width), low), ((choose.shape[0], width), wide)],
        grad, here, there, mods, member, choose,
        scratch=[pltpu.VMEM((rows, width), low)],
    )


def gradient_kernel(*refs):
    kept, sent = refs[-2:]
    rest = refs[:-2]
    half = kept.shape[1]
    block = 256
    first = 0
    for factor, own, other in [rest[i : i + 3] for i in range(0, len(rest), 3)]:
        rows = own.shape[0]
        base = first

        @pl.loop(0, factor.shape[1] // block)
        def _(index):
            at = pl.ds(pl.multiple_of(index * block, block), block)
            put = pl.ds(pl.multiple_of(base + index * block, block), block)
            turned = factor[:, at].T
            kept[put, :] = matmul(turned[:, :rows], own[:, :half]) + matmul(turned[:, rows:], other[:, :half])
            sent[put, :] = (
                matmul(turned[:, :rows], own[:, half:]) + matmul(turned[:, rows:], other[:, half:])
            ).astype(low)

        first += factor.shape[1]


def silu_of(value):
    return value / (1.0 + jnp.exp(-value))


def condition_kernel(classes, table, ada, cond_out, part_out):
    count = table.shape[0]
    hits = (classes[...] == lax.broadcasted_iota(jnp.int32, (classes.shape[0], count), 1)).astype(low)
    cond = matmul(hits, table[...])
    cond_out[...] = cond
    cond_low = silu_of(cond).astype(low)
    for layer in range(ada.shape[0]):
        part_out[layer] = matmul(cond_low, ada[layer])


def condition(classes, table, ada):
    count, width = classes.shape[0], table.shape[1]
    layers, _, columns = ada.shape
    return call(
        condition_kernel, [((count, width), wide), ((layers, count, columns), wide)], classes, table, ada
    )


def condition_back_kernel(*refs):
    cond, ada = refs[:2]
    grads, (ada_out, silu_out) = refs[2:-2], refs[-2:]
    cond_low = silu_of(cond[...]).astype(low)
    total = jnp.zeros(cond.shape, wide)
    for layer, grad in enumerate(grads):
        ada_out[layer] = contract_rows(cond_low, grad[...])
        total = total + contract_last(grad[...], ada[layer])
    silu_out[...] = total


def condition_back(cond, ada, grads):
    return call(condition_back_kernel, [(ada.shape, wide), (cond.shape, wide)], cond, ada, *grads)


def table_kernel(classes, cond, grad, out):
    value = cond[...]
    gate = 1.0 / (1.0 + jnp.exp(-value))
    slope = gate * (1.0 + value * (1.0 - gate))
    count = out.shape[0]
    hits = (classes[...] == lax.broadcasted_iota(jnp.int32, (count, classes.shape[1]), 0)).astype(wide)
    out[...] = jnp.dot(hits, grad[...] * slope, precision=lax.Precision.HIGHEST, preferred_element_type=wide)


def table_back(classes, cond, grad, count):
    return call(table_kernel, [((count, cond.shape[1]), wide)], classes, cond, grad)[0]


def gradient_blocks_kernel(order, *refs):
    out = refs[-1]
    rest = refs[:-1]
    count, _, span = out.shape
    block = 256
    first = 0
    for factor, own, other in [rest[i : i + 3] for i in range(0, len(rest), 3)]:
        rows = own.shape[0]
        base = first

        @pl.loop(0, factor.shape[1] // block)
        def _(index):
            at = pl.ds(pl.multiple_of(index * block, block), block)
            put = pl.ds(pl.multiple_of(base + index * block, block), block)
            turned = factor[:, at].T
            half = own.shape[1] // 2
            for side in range(2):
                columns = slice(side * half, (side + 1) * half)
                product = (matmul(turned[:, :rows], own[:, columns]) + matmul(turned[:, rows:], other[:, columns])).astype(low)
                for index_in in range(count // 2):
                    place = side * (count // 2) + index_in
                    out[order[place], put, :] = product[:, index_in * span : (index_in + 1) * span]

        first += factor.shape[1]


def gradient_blocks(order, *pairs):
    height = sum(left.shape[1] for left, _ in pairs)
    width = pairs[0][1][0].shape[1]
    count = order.shape[0]
    operands = [value for left, sides in pairs for value in (left, *sides)]
    if not paired(count):
        whole = [contract_rows(left, jnp.concatenate(sides, axis=0)) for left, sides in pairs]
        whole = jnp.concatenate(whole, axis=0).reshape(height, count, width // count)
        return jnp.swapaxes(whole, 0, 1).astype(low)
    return call(gradient_blocks_kernel, [((count, height, width // count), low)], order, *operands, scalars=1)[0]


def gradients(*pairs):
    height = sum(left.shape[1] for left, _ in pairs)
    half = pairs[0][1][0].shape[1] // 2
    operands = [value for left, sides in pairs for value in (left, *sides)]
    return call(gradient_kernel, [((height, half), wide), ((height, half), low)], *operands)


def on_device(
    tokens,
    out_grad,
    dest,
    lengths,
    classes,
    class_table,
    w_ada,
    w_qkv,
    head_scale,
    w_proj,
    w_fc1,
    w_fc2,
):
    rows, width = tokens.shape
    groups, shards = lax.axis_size("dp"), lax.axis_size("shard")
    layers = w_ada.shape[0]
    pack = rows * shards
    heads_here = head_scale.shape[1]
    items = lengths.shape[1]
    slots = rows // groups
    columns = w_ada.shape[2]
    me = lax.axis_index("shard")

    near = paired(groups)
    depth, span = w_qkv.shape[1], w_qkv.shape[3]
    flat = [w_qkv[layer].reshape(depth, -1) for layer in range(layers)]
    order = own_order(groups)
    def along(block):
        return lax.all_gather(block, "dp", axis=0, tiled=True, axis_index_groups=slow_groups)

    if near:
        mix_a = along(pack_mix(flat[0], w_proj, 0))

    if near:
        known = classes
        for offset in (1, 2, 4):
            known = jnp.concatenate([known, swap(known, "dp", offset)], axis=0)
        index = jnp.arange(groups, dtype=jnp.int32)
        found = (index[:, None] ^ index[None, :]) == lax.axis_index("dp")
        known = jnp.sum(jnp.where(found[:, :, None], known[None], 0), axis=1)
    else:
        known = lax.all_gather(classes, "dp", axis=0, tiled=True)
    all_classes = known.reshape(-1)

    def whole(own, hops, there, other, first, parts):
        size = own.shape[0]
        sources = [(0, 0), (1, 0), (2, 0), (3, 0), (4, first)] + [(5, i * size) for i in range(3)]
        return join([own, *hops, other, there], sources, parts)

    mix_parts = [(depth, 3 * span // 128, 0), (w_proj.shape[1], 1, 1)]
    fc1_parts = [(depth, w_fc1.shape[2] // 128, 0)]
    fc2_parts = [(w_fc2.shape[1], 1, 1)]
    if near:
        fc1_a = tie(pack_fc1(w_fc1, 0), all_classes)
        fc2_b = tie(w_fc2[0], all_classes)
        hops_a = straight(fc1_a)
        other_ab = swap(stack([fc1_a, fc2_b]), "dp", 1)
        mix_c, fc1_d, fc2_e = (
            along(tie(block, all_classes)) for block in (pack_mix(flat[1], w_proj, 1), pack_fc1(w_fc1, 1), w_fc2[1])
        )

    to_slots, to_rows = route(dest, rows)
    arrived = exchange(matmul(to_slots, tokens).astype(low).reshape(groups, slots, width), groups)
    packed = unpack(to_rows, arrived.reshape(rows, width), order)
    carried = jnp.concatenate([packed, swap(packed, "shard", 2)], axis=0).astype(wide)

    cond, part = condition(all_classes[:, None], class_table, w_ada)
    part = part + swap(part, "shard", 1)
    part = part + swap(part, "shard", 2)
    part = jnp.swapaxes(part.reshape(layers, groups, items, columns), 0, 1)
    upper = lax.reduce_precision(part, 8, 7)
    halves = jnp.stack([upper.astype(low), (part - upper).astype(low)], axis=1)
    halves = exchange(tie(halves.reshape(groups, 2 * layers * items, columns), packed), groups)
    modulation = spread(halves, order, layers, items, width)
    if near:
        modulation = tie(modulation, *hops_a, other_ab)
        there_m = swap(mix_a, "dp", 1)
        there_a = swap(stack(hops_a), "dp", 1)
        hops_b = straight(tie(fc2_b, modulation))

    def arrive(marker):
        grads_out = matmul(to_slots, tie(out_grad, marker)).astype(low).reshape(groups, slots, width)
        grads_out = exchange(grads_out, groups)
        grad_packed = unpack(to_rows, grads_out.reshape(rows, width), order)
        return jnp.concatenate([grad_packed, swap(grad_packed, "shard", 2)], axis=0).astype(wide)

    place = jnp.concatenate(
        [(me ^ offset) * rows + jnp.arange(rows, dtype=jnp.int32) for offset in (0, 2, 1, 3)]
    )
    member, level = pack_layout(lengths[0], place)
    layout = (member[:, None], level[:, None], member[None, :], level[None, :])
    here_member = member[: 2 * rows, None]
    choose = (jnp.arange(16, dtype=jnp.int32)[:, None] == member[None, : 2 * rows]).astype(low)
    scales = [head_scale[layer][None, :] for layer in range(layers)]
    mods = [modulation[layer] for layer in range(layers)]

    weights = [None] * layers
    saved = []
    first_low = enter(carried, mods[0], here_member, 2, 4)
    for layer in range(layers):
        if not near:
            qkv_full = lax.all_gather(flat[layer], "dp", axis=0, tiled=True)
            proj_full = lax.all_gather(w_proj[layer], "dp", axis=1, tiled=True)
            fc1_full = lax.all_gather(w_fc1[layer], "dp", axis=0, tiled=True)
            fc2_full = lax.all_gather(w_fc2[layer], "dp", axis=1, tiled=True)
        elif layer == 0:
            qkv_full, proj_full = join_pair(mix_a, there_m, order, mix_parts)
        else:
            qkv_full, proj_full = join_pair(mix_c, there_c, order, mix_parts)
        first = (first_low, swap(first_low, "shard", 1))
        if near and layer == 0:
            first = (first[0], tie(first[1], *hops_b))
            there_b = swap(stack(hops_b), "dp", 1)
        part_own, part_other, raw, heads_low, inverse = attend(
            *first, qkv_full, proj_full, scales[layer], layout, heads_here
        )
        here = gather_cores(part_own, part_other)
        if layer == 0:
            grad_carried = arrive(here)
        if near:
            here = tie(here, there_a if layer == 0 else there_d)
        there = swap(here, "shard", 2)
        if near and layer == 1:
            there_e = swap(tie(fc2_e, here), "dp", 1)
        attended = (here, there)
        middle, second_low = step(carried, *attended, mods[layer], mods[layer], here_member, 0, 3, 5)
        second = (second_low, swap(second_low, "shard", 1))
        if near and layer == 0:
            (fc1_full,) = whole(fc1_a, hops_a, there_a, other_ab, 0, fc1_parts)
            (fc2_full,) = whole(fc2_b, hops_b, there_b, other_ab, fc1_a.shape[0], fc2_parts)
        elif near:
            (fc1_full,) = join_pair(fc1_d, there_d, order, fc1_parts)
            (fc2_full,) = join_pair(fc2_e, there_e, order, fc2_parts)
        weights[layer] = (qkv_full, proj_full, fc1_full, fc2_full)
        part_own, part_other, hidden, activated = mlp(*second, fc1_full, fc2_full)
        here = gather_cores(part_own, part_other)
        there = swap(here, "shard", 2)
        if near and layer == 0:
            there_c = swap(tie(mix_c, here), "dp", 1)
        if layer == 0:
            there, grad_carried = lax.optimization_barrier((there, grad_carried))
        if near and layer == 0:
            there_d = swap(tie(fc1_d, there), "dp", 1)
        branch = (here, there)
        saved.append((carried, middle, first, raw, heads_low, inverse, attended, second, hidden, activated, branch))
        if layer + 1 < layers:
            carried, first_low = step(middle, *branch, mods[layer], mods[layer + 1], here_member, 1, 2, 4)
        else:
            carried = leave(middle, *branch, mods[layer], here_member, 1)

    mixed_out = repack(to_rows, carried, order).reshape(groups, slots, width)

    def give(layer):
        sums = collect(mod_sums[layer], width)
        return unspread(sums, swap(sums, "shard", 1), order, items, columns)

    layer_sums = [None] * layers
    scale_grads = [None] * layers
    mod_sums = [[None] * 6 for _ in range(layers)]
    grad_low, sums = first_back(grad_carried, *saved[-1][-1], mods[-1], here_member, choose, 1)
    mod_sums[-1][1] = (sums, 0)
    for layer in range(layers - 1, -1, -1):
        qkv_full, proj_full, fc1_full, fc2_full = weights[layer]
        carried_in, middle, first, raw, heads_low, inverse, attended, second, hidden, activated, branch = saved[layer]
        grad_branch = (grad_low, swap(grad_low, "shard", 1))
        if near:
            terms = gradients((activated, grad_branch))
            sums_fc2 = Sums(*terms)
            hidden = tie(hidden, *terms)
        part_own, part_other, grad_hidden = mlp_back(*grad_branch, hidden, fc1_full, fc2_full)
        here = gather_cores(part_own, part_other)
        there = swap(here, "shard", 2)
        if near:
            terms = gradients((tie(grad_hidden, here), second))
            there = tie(there, *terms, *([mixed_out] if layer else []))
            sums_fc1 = Sums(*terms)
            before = sums_fc2 if layer else layer_sums[1][0]
            there = tie(there, before.arrived)
            before.fold(True, there)
        else:
            sums_fc2 = WholeSums(gradient_blocks(order, (activated, grad_branch)))
            sums_fc1 = WholeSums(gradient_blocks(order, (grad_hidden, second)))
        grad_middle, grad_low, sums = step_back(
            middle, here, there, grad_carried, mods[layer], here_member, choose, 3, (mods[layer], 0, *attended)
        )
        mod_sums[layer][3], mod_sums[layer][5], mod_sums[layer][0] = ((sums, i * width) for i in range(3))
        grad_attended = (grad_low, swap(grad_low, "shard", 1))
        part_own, part_other, grad_projected, scale_grads[layer] = attend_back(
            *grad_attended, raw, inverse, qkv_full, proj_full, scales[layer], layout, heads_here
        )
        here = gather_cores(part_own, part_other)
        there = swap(here, "shard", 2)
        if near:
            terms = gradients((tie(heads_low, here), grad_attended), (grad_projected, first))
            there = tie(there, *terms)
            sums_attn = Sums(*terms)
            before = sums_fc1 if layer else sums_fc2
            there = tie(there, before.arrived)
            before.fold(True, there)
        else:
            blocks_attn = gradient_blocks(order, (heads_low, grad_attended), (grad_projected, first))
            sums_attn = WholeSums(blocks_attn)
        if layer > 0:
            grad_carried, grad_low, sums = step_back(
                carried_in, here, there, grad_middle, mods[layer], here_member, choose, 2, (mods[layer - 1], 1, *saved[layer - 1][-1])
            )
            mod_sums[layer - 1][1] = (sums, 2 * width)
        else:
            grad_carried, sums = step_back(carried_in, here, there, grad_middle, mods[layer], here_member, choose, 2)
        mod_sums[layer][2], mod_sums[layer][4] = (sums, 0), (sums, width)
        layer_sums[layer] = (sums_attn, sums_fc1, sums_fc2)
    if near:
        layer_sums[0][1].fold(True, grad_carried)
        layer_sums[0][0].fold(False, grad_carried)

    grads_back = repack(to_rows, grad_carried, order).reshape(groups, slots, width)
    sent = jnp.stack([give(layer) for layer in range(layers)], axis=1).reshape(groups, layers * items * columns)
    if sent.shape[1] % width:
        back = exchange(jnp.concatenate([mixed_out, grads_back], axis=1), groups)
        mods_back = exchange(sent, groups)
    else:
        sent = sent.reshape(groups, -1, width)
        back = exchange(jnp.concatenate([mixed_out, grads_back, sent], axis=1), groups)
        mods_back = back[:, 2 * slots :]
    mixed_back, grads_back = back[:, :slots], back[:, slots : 2 * slots]
    mods_back = mods_back.reshape(groups, layers, items, columns)
    mods_back = [mods_back[:, layer] for layer in range(layers)]

    mixed = contract_rows(to_slots, mixed_back.reshape(rows, width)).astype(low)
    tokens_grad = contract_rows(to_slots, grads_back.reshape(rows, width)).astype(low)
    ada_grad, grad_silu = condition_back(
        cond, w_ada, [back.reshape(groups * items, columns) for back in mods_back]
    )
    logs = jnp.pad(jnp.stack(scale_grads).reshape(1, -1), ((0, 7), (0, cond.shape[1] - layers * heads_here)))
    summed = jnp.concatenate([grad_silu, logs], axis=0)
    if paired(groups):
        for offset in (1, 2, 4):
            summed = summed + swap(summed, "dp", offset)
    else:
        summed = lax.psum(summed, "dp")
    grad_silu = summed[: cond.shape[0]]
    scale_grad = summed[cond.shape[0], : layers * heads_here].reshape(layers, heads_here)
    table_grad = table_back(all_classes[None, :], cond, grad_silu, class_table.shape[0])
    spanned = w_proj.shape[1]
    layer_grads = []
    for layer in range(layers):
        attn, fc1, fc2 = (sums.total(grad_carried) for sums in layer_sums[layer])
        layer_grads.append((attn[spanned:].T.reshape(w_qkv.shape[1:]), attn[:spanned], fc1.T, fc2))
    qkv_grad, proj_grad, fc1_grad, fc2_grad = (
        jnp.stack([layer_grads[layer][i] for layer in range(layers)]) for i in range(4)
    )
    return (
        mixed,
        tokens_grad,
        table_grad,
        ada_grad,
        qkv_grad,
        scale_grad,
        proj_grad,
        fc1_grad,
        fc2_grad,
    )


def solution(mesh):
    placed = (
        P(("dp", "shard"), None),
        P(("dp", "shard"), None),
        P(None, "shard", None),
        P("dp", None),
        P("dp", None),
        P(None, "shard"),
        P(None, "shard", "dp"),
        P(None, "dp", None, "shard"),
        P(None, "shard"),
        P(None, "shard", "dp"),
        P(None, "dp", "shard"),
        P(None, "shard", "dp"),
    )
    return jax.shard_map(
        on_device,
        mesh=mesh,
        in_specs=placed,
        out_specs=(
            P(("dp", "shard"), None),
            P(("dp", "shard"), None),
            P(None, "shard"),
            P(None, "shard", "dp"),
            P(None, "dp", None, "shard"),
            P(None, "shard"),
            P(None, "shard", "dp"),
            P(None, "dp", "shard"),
            P(None, "shard", "dp"),
        ),
        check_vma=False,
    )
```

```python
import functools

import jax
import jax.numpy as jnp
from jax import lax
from jax.experimental import pallas as pl
from jax.experimental.pallas import tpu as pltpu
from jax.sharding import PartitionSpec as P

epsilon = 1e-06
level_ends = (1, 5, 14, 30, 55, 91, 155, 255, 424, 680)
wide = jnp.float32
low = jnp.bfloat16
root = 0.7978845608028654
cubic = 0.044715


def matmul(left, right):
    return jnp.dot(left, right, preferred_element_type=wide)


def contract_rows(left, right):
    return lax.dot_general(left, right, (((0,), (0,)), ((), ())), preferred_element_type=wide)


def contract_last(left, right):
    return lax.dot_general(left, right, (((1,), (1,)), ((), ())), preferred_element_type=wide)


def swap(value, axis, offset):
    size = lax.axis_size(axis)
    return lax.ppermute(value, axis, [(i, i ^ offset) for i in range(size)])


def tie(value, *others):
    return lax.optimization_barrier((value, others))[0]


slow_groups = [[0, 2, 4, 6], [1, 3, 5, 7]]


def paired(groups):
    return groups == 8


def own_order(groups):
    here = lax.axis_index("dp")
    if not paired(groups):
        return jnp.arange(groups, dtype=jnp.int32)
    place = jnp.arange(groups, dtype=jnp.int32)
    return (lax.rem(here // 2 + 4 - place % 4, 4) * 2 + (here % 2 ^ place // 4)).astype(jnp.int32)


def straight(block):
    return [lax.ppermute(block, "dp", [(i, (i + 2 * back) % 8) for i in range(8)]) for back in (1, 2, 3)]


def columns_of(piece, out, first):
    depth, width = piece.shape
    for index in range(width // 128):
        out[first + index * depth : first + (index + 1) * depth, :] = piece[:, index * 128 : (index + 1) * 128]


def pack_mix_kernel(qkv, proj, *refs, layer):
    out = refs[-1]
    columns_of(qkv[...], out, 0)
    first = qkv.shape[0] * qkv.shape[1] // 128
    out[first : first + proj.shape[1], :] = proj[layer]
    if len(refs) > 1:
        out[first + proj.shape[1] :, :] = refs[0][layer]


def pack_mix(qkv, proj, layer, *more):
    height = qkv.shape[0] * qkv.shape[1] // 128 + proj.shape[1] + sum(value.shape[1] for value in more)
    return call(functools.partial(pack_mix_kernel, layer=layer), [((height, 128), low)], qkv, proj, *more)[0]


def pack_fc1_kernel(fc1, out, *, layer):
    columns_of(fc1[layer], out, 0)


def pack_fc1(fc1, layer):
    height = fc1.shape[1] * fc1.shape[2] // 128
    return call(functools.partial(pack_fc1_kernel, layer=layer), [((height, 128), low)], fc1)[0]


def pack_pair_kernel(fc1, fc2, out, *, layer):
    columns_of(fc1[layer], out, 0)
    out[fc2.shape[1] :, :] = fc2[layer]


def pack_pair(fc1, fc2, layer):
    return call(functools.partial(pack_pair_kernel, layer=layer), [((2 * fc2.shape[1], 128), low)], fc1, fc2)[0]


def stack_kernel(*refs):
    out = refs[-1]
    size = refs[0].shape[0]
    for index, ref in enumerate(refs[:-1]):
        out[index * size : (index + 1) * size, :] = ref[...]


def stack(blocks):
    size = blocks[0].shape[0]
    return call(stack_kernel, [((size * len(blocks), 128), low)], *blocks)[0]


def put_block(read, place, outs, parts):
    first = 0
    for out, (depth, columns, axis) in zip(outs, parts):
        for index in range(columns):
            piece = read(first, depth)
            first += depth
            if axis == 0:
                out[place * depth : (place + 1) * depth, index * 128 : (index + 1) * 128] = piece
            else:
                out[:, place * 128 : (place + 1) * 128] = piece


def join_kernel(*refs, sources, parts):
    outs = refs[-len(parts) :]
    for place, (ref, base) in enumerate(sources):
        put_block(lambda first, depth: refs[ref][base + first : base + first + depth, :], place, outs, parts)


def pair_kernel(order, here, there, *outs, parts):
    size = here.shape[0] // 4
    for place in range(8):
        base = (order[place] // 2) * size
        blocks = there if place // 4 else here
        put_block(
            lambda first, depth: blocks[pl.ds(pl.multiple_of(base + first, 128), depth), :], place, outs, parts
        )


def join_pair(here, there, order, parts):
    return call(functools.partial(pair_kernel, parts=parts), joined_shapes(8, parts), order, here, there, scalars=1)


def order_kernel(order, blocks, *outs, parts):
    size = blocks.shape[0] // order.shape[0]
    for place in range(order.shape[0]):
        base = order[place] * size
        put_block(
            lambda first, depth: blocks[pl.ds(pl.multiple_of(base + first, 128), depth), :], place, outs, parts
        )


def joined_shapes(count, parts):
    return [((depth, 128 * count) if axis else (depth * count, columns * 128), low) for depth, columns, axis in parts]


def join(arrays, sources, parts):
    return call(
        functools.partial(join_kernel, sources=sources, parts=parts), joined_shapes(len(sources), parts), *arrays
    )


def join_ordered(blocks, order, parts):
    return call(
        functools.partial(order_kernel, parts=parts), joined_shapes(order.shape[0], parts), order, blocks, scalars=1
    )


def unpack_kernel(order, to_rows, arrived, out, kept):
    kept[...] = matmul(to_rows[...], arrived[...]).astype(low)
    span = out.shape[1] // order.shape[0]
    for place in range(order.shape[0]):
        out[:, place * span : (place + 1) * span] = kept[:, pl.ds(pl.multiple_of(order[place] * span, span), span)]


def unpack(to_rows, arrived, order):
    if not paired(order.shape[0]):
        return matmul(to_rows, arrived).astype(low)
    shape = (to_rows.shape[0], arrived.shape[1])
    return call(
        unpack_kernel, [(shape, low)], order, to_rows, arrived, scratch=[pltpu.VMEM(shape, low)], scalars=1
    )[0]


def repack_kernel(order, to_rows, value, out, kept):
    rows, span = out.shape[0], out.shape[1] // order.shape[0]
    for place in range(order.shape[0]):
        at = pl.ds(pl.multiple_of(order[place] * span, span), span)
        kept[:, at] = value[:rows, place * span : (place + 1) * span].astype(low)
    out[...] = contract_rows(to_rows[...], kept[...]).astype(low)


def repack(to_rows, value, order):
    shape = (to_rows.shape[0], value.shape[1])
    if not paired(order.shape[0]):
        return matmul(to_rows.T, value[: shape[0]].astype(low)).astype(low)
    return call(
        repack_kernel, [(shape, low)], order, to_rows, value, scratch=[pltpu.VMEM(shape, low)], scalars=1
    )[0]


def collect_kernel(*refs, offsets):
    out = refs[-1]
    lines, width = out.shape[0], out.shape[1] // 6
    for part, (ref, first) in enumerate(zip(refs[:-1], offsets)):
        out[:, part * width : (part + 1) * width] = ref[:lines, first : first + width]


def collect(parts, width):
    return call(
        functools.partial(collect_kernel, offsets=[first for _, first in parts]),
        [((8, 6 * width), wide)],
        *[value for value, _ in parts],
    )[0]


def unspread_kernel(order, own, other, out):
    count, _, columns = out.shape
    blocks = columns // 128
    for part in range(6):
        for place in range(count):
            first = (part * count + place) * 128
            block = order[place] + part * count
            at = pl.ds(pl.multiple_of(lax.rem(block, blocks) * 128, 128), 128)
            out[block // blocks, :, at] = (own[:, first : first + 128] + other[:, first : first + 128]).astype(low)


def unspread(own, other, order, items, columns):
    count = order.shape[0]
    if paired(count):
        return call(unspread_kernel, [((count, own.shape[0], columns), low)], order, own, other, scalars=1)[0][:, :items]
    return jnp.swapaxes((own + other).astype(low)[:items].reshape(items, count, columns), 0, 1)


def spread_kernel(order, arrived, out):
    count, lines, columns = arrived.shape
    layers, parts, items, _ = out.shape
    blocks = columns // 128
    for part in range(parts):
        for place in range(count):
            block = order[place] + part * count
            source = block // blocks
            at = pl.ds(pl.multiple_of(lax.rem(block, blocks) * 128, 128), 128)
            rows = arrived[source, :, at].astype(wide)
            total = rows[: lines // 2] + rows[lines // 2 :]
            for layer in range(layers):
                out[layer, part, :, place * 128 : (place + 1) * 128] = total[layer * items : (layer + 1) * items]


def spread(arrived, order, layers, items, width):
    count, lines, columns = arrived.shape
    if paired(count):
        return call(spread_kernel, [((layers, 6, items, width), wide)], order, arrived, scalars=1)[0]
    halves = arrived.astype(wide).reshape(count, 2, layers, items, columns)
    whole = jnp.transpose(halves[:, 0] + halves[:, 1], (1, 2, 0, 3)).reshape(layers, items, 6, width)
    return jnp.swapaxes(whole, 1, 2)


def fold_kernel(slow, kept, arrived, out):
    span = out.shape[2]
    for back in range(4):
        columns = slice(back * span, (back + 1) * span)
        out[lax.rem(slow[0] + 4 - back, 4)] = (kept[:, columns].astype(wide) + arrived[:, columns].astype(wide)).astype(low)


def fold(kept, arrived, slow):
    height, half = kept.shape
    return call(fold_kernel, [((4, height, half // 4), low)], slow, kept, arrived, scalars=1)[0]


class Sums:
    def __init__(self, kept, sent):
        self.kept = kept
        self.arrived = swap(sent, "dp", 1)

    def fold(self, along, marker):
        if along:
            slow = (lax.axis_index("dp") // 2).astype(jnp.int32).reshape(1)
            blocks = fold(self.kept, tie(self.arrived, marker), slow)
            self.blocks = lax.psum_scatter(
                blocks, "dp", scatter_dimension=0, axis_index_groups=slow_groups, tiled=True
            )
            return tie(marker, blocks)
        self.blocks = None
        total = self.kept.astype(wide) + tie(self.arrived, marker).astype(wide)
        span = total.shape[1] // 4
        self.parts = [total[:, i * span : (i + 1) * span] for i in range(4)]
        for back in (1, 2, 3):
            pairs = [(i, (i + 8 - 2 * back) % 8) for i in range(8)]
            self.parts[back] = lax.ppermute(self.parts[back].astype(low), "dp", pairs)

    def total(self, marker):
        if self.blocks is not None:
            return tie(self.blocks, marker).reshape(self.blocks.shape[1:]).astype(wide)
        parts = [tie(part, marker) for part in self.parts]
        return parts[0] + parts[1].astype(wide) + parts[2].astype(wide) + parts[3].astype(wide)


class WholeSums:
    def __init__(self, blocks):
        self.arrived = blocks
        self.result = lax.psum_scatter(blocks, "dp", scatter_dimension=0, tiled=True)

    def fold(self):
        pass

    def total(self, marker):
        return tie(self.result, marker).reshape(self.result.shape[1:]).astype(wide)


def gather_cores_kernel(own, first, second, out):
    half = first.shape[0]
    out[:half, :] = (own[:half, :] + first[...].astype(wide)).astype(low)
    out[half:, :] = (own[half:, :] + second[...].astype(wide)).astype(low)


def gather_cores(part_own, parts_other):
    arrived = [swap(part, "shard", 1) for part in parts_other]
    return call(gather_cores_kernel, [(part_own.shape, low)], part_own, *arrived)[0]


def route(dest, rows):
    table = dest[:, 0, :]
    groups = table.shape[0]
    capacity = rows // groups
    here = lax.axis_index("dp")
    own = lax.dynamic_index_in_dim(table, here, 0, keepdims=False)
    pack = own // rows
    index = jnp.arange(rows, dtype=jnp.int32)
    earlier = index[None, :] < index[:, None]
    rank = jnp.sum((earlier & (pack[None, :] == pack[:, None])).astype(jnp.int32), axis=1)
    slot = pack * capacity + rank
    to_slots = (slot[None, :] == index[:, None]).astype(low)
    mine = table // rows == here
    rank_in = jnp.sum((earlier[None] & mine[:, None, :]).astype(jnp.int32), axis=2)
    slot_in = jnp.arange(groups, dtype=jnp.int32)[:, None] * capacity + rank_in
    slot_in = jnp.where(mine, slot_in, rows).reshape(-1)
    row_in = (table % rows).reshape(-1)
    by_row = (row_in[None, :] == index[:, None]).astype(low)
    by_slot = (slot_in[None, :] == index[:, None]).astype(low)
    to_rows = contract_last(by_row, by_slot).astype(low)
    return to_slots, to_rows


def exchange(value, groups):
    return lax.all_to_all(value, "dp", split_axis=0, concat_axis=0, tiled=True)


def pack_layout(lengths, place):
    ends = jnp.cumsum(lengths)
    starts = ends - lengths
    member = jnp.sum((place[:, None] >= ends[None, :]).astype(jnp.int32), axis=1)
    onehot = member[:, None] == jnp.arange(lengths.shape[0], dtype=jnp.int32)[None, :]
    start = jnp.sum(jnp.where(onehot, starts[None, :], jnp.int32(0)), axis=1)
    bounds = jnp.array(level_ends, dtype=jnp.int32)
    level = jnp.sum(((place - start)[:, None] >= bounds[None, :]).astype(jnp.int32), axis=1)
    return member, level


grant = 24
stripe = 64


def call(kernel, outs, *operands, scratch=(), scalars=0, cost=1):
    spec = pl.BlockSpec(memory_space=pltpu.VMEM)
    return pl.pallas_call(
        kernel,
        out_shape=[jax.ShapeDtypeStruct(shape, kind) for shape, kind in outs],
        in_specs=[pl.BlockSpec(memory_space=pltpu.SMEM)] * scalars + [spec] * (len(operands) - scalars),
        out_specs=[spec] * len(outs),
        scratch_shapes=list(scratch),
        cost_estimate=pl.CostEstimate(flops=cost, bytes_accessed=1, transcendentals=0),
        compiler_params=pltpu.CompilerParams(vmem_limit_bytes=grant << 20),
    )(*operands)


def pick(member, table):
    items = table.shape[0]
    result = table[items - 1 : items, :]
    for item in range(items - 2, -1, -1):
        result = jnp.where(member == item, table[item : item + 1, :], result)
    return result


def normed(value):
    centered = value - jnp.mean(value, axis=-1, keepdims=True)
    inverse = lax.rsqrt(jnp.mean(centered * centered, axis=-1, keepdims=True) + epsilon)
    return centered * inverse, inverse


def stripes(rows, body):
    @pl.loop(0, rows // stripe)
    def _(index):
        first = pl.multiple_of(index * stripe, stripe)
        body(pl.ds(first, stripe), pl.ds(pl.multiple_of(lax.rem(first + rows // 2, rows), stripe), stripe))


def enter_kernel(value, mods, member, out, *, scale, shift):
    def body(at, _):
        who = member[at, :]
        unit, _inverse = normed(value[at, :])
        out[at, :] = (unit * (1.0 + pick(who, mods[scale])) + pick(who, mods[shift])).astype(low)

    stripes(value.shape[0], body)


def enter(value, mods, member, scale, shift):
    return call(
        functools.partial(enter_kernel, scale=scale, shift=shift), [(value.shape, low)], value, mods, member
    )[0]


def step_kernel(value, here, there, mods_gain, mods, member, out, low_out, *, gain, scale, shift):
    def body(at, across):
        who = member[at, :]
        branch = here[at, :].astype(wide) + there[across, :].astype(wide)
        total = value[at, :] + pick(who, mods_gain[gain]) * branch
        out[at, :] = total
        unit, _inverse = normed(total)
        low_out[at, :] = (unit * (1.0 + pick(who, mods[scale])) + pick(who, mods[shift])).astype(low)

    stripes(value.shape[0], body)


def step(value, here, there, mods_gain, mods, member, gain, scale, shift):
    return call(
        functools.partial(step_kernel, gain=gain, scale=scale, shift=shift),
        [(value.shape, wide), (value.shape, low)],
        value, here, there, mods_gain, mods, member,
    )


def leave_kernel(value, here, there, mods, member, out, *, gain):
    def body(at, across):
        branch = here[at, :].astype(wide) + there[across, :].astype(wide)
        out[at, :] = value[at, :] + pick(member[at, :], mods[gain]) * branch

    stripes(value.shape[0], body)


def leave(value, here, there, mods, member, gain):
    return call(
        functools.partial(leave_kernel, gain=gain), [(value.shape, wide)], value, here, there, mods, member
    )[0]


def put_part(targets, at, value):
    if len(targets) == 1:
        targets[0][at, :] = value.astype(targets[0].dtype)
        return
    half = targets[0].shape[0]
    for index, target in enumerate(targets):
        first, last = max(at.start, index * half), min(at.stop, (index + 1) * half)
        if first < last:
            target[first - index * half : last - index * half, :] = value[first - at.start : last - at.start].astype(target.dtype)


def mlp_kernel(own, other, fc1, fc2, part_own, part_a, part_b, slope_out, act_out):
    half = own.shape[0]
    for place, source, target in ((0, own, (part_own,)), (1, other, (part_a, part_b))):
        for index in range(half // 256):
            at = slice(index * 256, (index + 1) * 256)
            put = slice(place * half + index * 256, place * half + (index + 1) * 256)
            hidden = matmul(source[at, :], fc1[...])
            square = hidden * hidden
            bent = jnp.tanh(hidden * (root + (root * cubic) * square))
            share = 0.5 + 0.5 * bent
            activated = (hidden * share).astype(low)
            slope = share + (hidden * (1.0 - bent * bent)) * (0.5 * root + (1.5 * root * cubic) * square)
            slope_out[put, :] = slope.astype(low)
            act_out[put, :] = activated
            put_part(target, at, matmul(activated, fc2[...]))


def mlp(own, other, fc1, fc2):
    half, width = own.shape
    units = fc1.shape[1]
    return call(
        mlp_kernel,
        [((half, width), wide), ((half // 2, width), low), ((half // 2, width), low), ((2 * half, units), low), ((2 * half, units), low)],
        own, other, fc1, fc2,
    )


def mlp_back_kernel(own, other, slope, fc1, fc2, part_own, part_a, part_b, grad_out):
    half = own.shape[0]
    for place, source, target in ((0, own, (part_own,)), (1, other, (part_a, part_b))):
        for index in range(half // 256):
            at = slice(index * 256, (index + 1) * 256)
            put = slice(place * half + index * 256, place * half + (index + 1) * 256)
            grad_activated = contract_last(source[at, :], fc2[...])
            grad_hidden = (grad_activated * slope[put, :].astype(wide)).astype(low)
            grad_out[put, :] = grad_hidden
            put_part(target, at, contract_last(grad_hidden, fc1[...]))


def mlp_back(own, other, slope, fc1, fc2):
    half, width = own.shape
    return call(
        mlp_back_kernel,
        [((half, width), wide), ((half // 2, width), low), ((half // 2, width), low), (slope.shape, low)],
        own, other, slope, fc1, fc2,
    )


def heads_of(shape, heads):
    lane = lax.broadcasted_iota(jnp.int32, shape, 1)
    span = shape[1] // heads
    return [(lane >= head * span) & (lane < (head + 1) * span) for head in range(heads)]


def head_sums(value, masks):
    return [jnp.sum(jnp.where(mask, value, 0.0), axis=1, keepdims=True) for mask in masks]


def by_head(columns, masks):
    result = columns[-1]
    for column, mask in zip(columns[-2::-1], masks[-2::-1]):
        result = jnp.where(mask, column, result)
    return result


def allowed_at(member, level, member_row, level_row, at):
    return (member[at, :] == member_row[...]) & (level_row[...] <= level[at, :])


def attend_kernel(
    own, other, qkv, proj, scale, member, level, member_row, level_row,
    part_own, part_a, part_b, kept, inverse_out, *, heads,
):
    half = own.shape[0]
    span = qkv.shape[1] // 3
    block = 256
    queries, keys, values, heads_out = (kept.at[:, i * span : (i + 1) * span] for i in range(4))
    for place, source in ((0, own), (1, other)):
        @pl.loop(0, half // block)
        def _(index):
            at = pl.ds(pl.multiple_of(index * block, block), block)
            put = pl.ds(pl.multiple_of(place * half + index * block, block), block)
            projected = matmul(source[at, :], qkv[...])
            masks = heads_of((block, span), heads)
            query, key = projected[:, :span], projected[:, span : 2 * span]
            inverse_q = [lax.rsqrt(total + epsilon) for total in head_sums(query * query, masks)]
            inverse_k = [lax.rsqrt(total + epsilon) for total in head_sums(key * key, masks)]
            rises = [jnp.exp(scale[:, head : head + 1]) for head in range(heads)]
            queries[put, :] = (query * by_head([i * a for i, a in zip(inverse_q, rises)], masks)).astype(low)
            keys[put, :] = (key * by_head(inverse_k, masks)).astype(low)
            values[put, :] = projected[:, 2 * span :].astype(low)
            inverse_out[put, : 2 * heads] = jnp.concatenate(inverse_q + inverse_k, axis=1)

    rows = 2 * half
    for place, target in ((0, (part_own,)), (1, (part_a, part_b))):
        for index in range(half // block):
            at = slice(index * block, (index + 1) * block)
            put = slice(place * half + index * block, place * half + (index + 1) * block)
            allowed = allowed_at(member, level, member_row, level_row, put)
            query = queries[put, :]
            masks = heads_of((block, span), heads)
            wide_masks = heads_of((rows, span), heads)
            outputs = jnp.zeros((block, span), wide)
            inverses = []
            for head in range(heads):
                scores = contract_last(jnp.where(masks[head], query, jnp.zeros_like(query)), keys[...])
                raised = jnp.where(allowed, jnp.exp(scores - jnp.exp(scale[:, head : head + 1])), 0.0)
                inverse = 1.0 / jnp.sum(raised, axis=1, keepdims=True)
                inverses.append(inverse)
                weights = (raised * inverse).astype(low)
                outputs = outputs + matmul(weights, jnp.where(wide_masks[head], values[...], jnp.zeros((), low)))
            inverse_out[put, 2 * heads :] = jnp.concatenate(inverses, axis=1)
            outputs = outputs.astype(low)
            heads_out[put, :] = outputs
            put_part(target, at, matmul(outputs, proj[...]))


def attend(own, other, qkv, proj, scale, layout, heads):
    half, width = own.shape
    rows, span = 2 * half, qkv.shape[1] // 3
    return call(
        functools.partial(attend_kernel, heads=heads),
        [((half, width), wide), ((half // 2, width), low), ((half // 2, width), low)] + [((rows, 4 * span), low), ((rows, 3 * heads), wide)],
        own, other, qkv, proj, scale, *layout,
    )


def attend_back_kernel(
    own, other, kept, inverse_in, qkv, proj, scale, member, level, member_row, level_row,
    part_own, part_a, part_b, grad_out, log_out,
    grads, grad_queries, key_sums_t, value_sums_t, *, heads,
):
    half = own.shape[0]
    rows = 2 * half
    span = qkv.shape[1] // 3
    block = 256
    queries, keys, values = (kept.at[:, i * span : (i + 1) * span] for i in range(3))
    grads[:half, :] = contract_last(own[...], proj[...]).astype(low)
    grads[half:, :] = contract_last(other[...], proj[...]).astype(low)
    key_sums_t[...] = jnp.zeros_like(key_sums_t)
    value_sums_t[...] = jnp.zeros_like(value_sums_t)
    deep = span // heads
    step_rows = 256

    @pl.loop(0, rows // step_rows)
    def _(index):
        put = pl.ds(pl.multiple_of(index * step_rows, step_rows), step_rows)
        allowed = allowed_at(member, level, member_row, level_row, put)
        query, grad = queries[put, :], grads[put, :]
        query_t, grad_t = query.astype(wide).T.astype(low), grad.astype(wide).T.astype(low)
        masks = heads_of((step_rows, span), heads)
        wide_masks = heads_of((rows, span), heads)
        outputs = jnp.zeros((step_rows, span), wide)
        for head in range(heads):
            scores = contract_last(jnp.where(masks[head], query, jnp.zeros_like(query)), keys[...])
            raised = jnp.where(allowed, jnp.exp(scores - jnp.exp(scale[:, head : head + 1])), 0.0)
            weights = raised * inverse_in[put, 2 * heads + head : 2 * heads + head + 1]
            grad_weights = contract_last(jnp.where(masks[head], grad, jnp.zeros_like(grad)), values[...])
            inner = jnp.sum(weights * grad_weights, axis=1, keepdims=True)
            grad_scores = (weights * (grad_weights - inner)).astype(low)
            outputs = outputs + matmul(grad_scores, jnp.where(wide_masks[head], keys[...], jnp.zeros((), low)))
            these = slice(head * deep, (head + 1) * deep)
            key_sums_t[these, :] += matmul(query_t[these, :], grad_scores)
            value_sums_t[these, :] += matmul(grad_t[these, :], weights.astype(low))
        grad_queries[put, :] = outputs

    log_out[...] = jnp.zeros_like(log_out)
    grad_keys = key_sums_t[...].T
    grad_out[:, 2 * span :] = value_sums_t[...].T.astype(low)
    rises = [jnp.exp(scale[:, head : head + 1]) for head in range(heads)]
    for place, target in ((0, (part_own,)), (1, (part_a, part_b))):
        for index in range(half // block):
            put = slice(place * half + index * block, place * half + (index + 1) * block)
            at = slice(index * block, (index + 1) * block)
            masks = heads_of((block, span), heads)
            query, key = queries[put, :].astype(wide), keys[put, :].astype(wide)
            grad_query, grad_key = grad_queries[put, :], grad_keys[put, :]
            inverse = [inverse_in[put, i : i + 1] for i in range(2 * heads)]
            dots_q, dots_k = head_sums(query * grad_query, masks), head_sums(key * grad_key, masks)
            log_out[...] += jnp.concatenate([jnp.sum(x, axis=0, keepdims=True) for x in dots_q], axis=1)
            first = by_head([a * i for a, i in zip(rises, inverse[:heads])], masks)
            second = by_head([d * i / a for a, d, i in zip(rises, dots_q, inverse[:heads])], masks)
            grad_out[put, :span] = (grad_query * first - query * second).astype(low)
            first = by_head(inverse[heads:], masks)
            second = by_head([d * i for d, i in zip(dots_k, inverse[heads:])], masks)
            grad_out[put, span : 2 * span] = (grad_key * first - key * second).astype(low)
            put_part(target, at, contract_last(grad_out[put, :], qkv[...]))


def attend_back(own, other, kept, qkv, proj, scale, layout, heads):
    half, width = own.shape
    rows, span = 2 * half, qkv.shape[1] // 3
    return call(
        functools.partial(attend_back_kernel, heads=heads),
        [((half, width), wide), ((half // 2, width), low), ((half // 2, width), low), ((rows, 3 * span), low), ((1, heads), wide)],
        own, other, *kept, qkv, proj, scale, *layout,
        scratch=[pltpu.VMEM((rows, span), low), pltpu.VMEM((rows, span), wide)]
        + [pltpu.VMEM((span, rows), wide), pltpu.VMEM((span, rows), wide)],
    )


def step_back_kernel(
    value, here, there, grad, mods, mods_gain, branch_here, branch_there, member, choose,
    grad_out, low_out, sums_out, terms, *, scale, gain,
):
    width = value.shape[1]

    def body(at, across):
        who = member[at, :]
        unit, inverse = normed(value[at, :])
        arrived = here[at, :].astype(wide) + there[across, :].astype(wide)
        scaled = arrived * (1.0 + pick(who, mods[scale]))
        total = grad[at, :] + inverse * (
            scaled
            - jnp.mean(scaled, axis=-1, keepdims=True)
            - unit * jnp.mean(scaled * unit, axis=-1, keepdims=True)
        )
        grad_out[at, :] = total
        terms[at, : width] = (arrived * unit).astype(low)
        terms[at, width : 2 * width] = arrived.astype(low)
        if gain is not None:
            branch = branch_here[at, :].astype(wide) + branch_there[across, :].astype(wide)
            terms[at, 2 * width :] = (total * branch).astype(low)
            low_out[at, :] = (total * pick(who, mods_gain[gain])).astype(low)

    stripes(value.shape[0], body)
    sums_out[...] = matmul(choose[...], terms[...])


def last_back_kernel(value, here, there, grad, mods, member, choose, grad_out, sums_out, terms, *, scale):
    step_back_kernel(
        value, here, there, grad, mods, None, None, None, member, choose,
        grad_out, None, sums_out, terms, scale=scale, gain=None,
    )


def step_back(value, here, there, grad, mods, member, choose, scale, before=None):
    rows, width = value.shape
    lines = choose.shape[0]
    if before is None:
        return call(
            functools.partial(last_back_kernel, scale=scale),
            [((rows, width), wide), ((lines, 2 * width), wide)],
            value, here, there, grad, mods, member, choose,
            scratch=[pltpu.VMEM((rows, 2 * width), low)],
        )
    mods_gain, gain, branch_here, branch_there = before
    return call(
        functools.partial(step_back_kernel, scale=scale, gain=gain),
        [((rows, width), wide), ((rows, width), low), ((lines, 3 * width), wide)],
        value, here, there, grad, mods, mods_gain, branch_here, branch_there, member, choose,
        scratch=[pltpu.VMEM((rows, 3 * width), low)],
    )


def first_back_kernel(grad, here, there, mods, member, choose, low_out, sums_out, terms, *, gain):
    def body(at, across):
        branch = here[at, :].astype(wide) + there[across, :].astype(wide)
        terms[at, :] = (grad[at, :] * branch).astype(low)
        low_out[at, :] = (grad[at, :] * pick(member[at, :], mods[gain])).astype(low)

    stripes(grad.shape[0], body)
    sums_out[...] = matmul(choose[...], terms[...])


def first_back(grad, here, there, mods, member, choose, gain):
    rows, width = grad.shape
    return call(
        functools.partial(first_back_kernel, gain=gain),
        [((rows, width), low), ((choose.shape[0], width), wide)],
        grad, here, there, mods, member, choose,
        scratch=[pltpu.VMEM((rows, width), low)],
    )


def gradient_kernel(*refs, spans):
    kept, sent = refs[-2:]
    rest = refs[:-2]
    half = kept.shape[1]
    first = 0
    for (begin, end), factor, own, other in [(spans[i // 3], *rest[i : i + 3]) for i in range(0, len(rest), 3)]:
        rows = own.shape[0]
        put = slice(first, first + end - begin)
        turned = factor[:, begin:end].T
        kept[put, :] = (matmul(turned[:, :rows], own[:, :half]) + matmul(turned[:, rows:], other[:, :half])).astype(low)
        sent[put, :] = (matmul(turned[:, :rows], own[:, half:]) + matmul(turned[:, rows:], other[:, half:])).astype(low)
        first += end - begin


def silu_of(value):
    return value / (1.0 + jnp.exp(-value))


def condition_kernel(classes, table, ada, cond_out, part_out):
    count = table.shape[0]
    hits = (classes[...] == lax.broadcasted_iota(jnp.int32, (classes.shape[0], count), 1)).astype(low)
    cond = matmul(hits, table[...])
    cond_out[...] = cond
    cond_low = silu_of(cond).astype(low)
    for layer in range(ada.shape[0]):
        part_out[layer] = matmul(cond_low, ada[layer])


def condition(classes, table, ada):
    count, width = classes.shape[0], table.shape[1]
    layers, _, columns = ada.shape
    return call(
        condition_kernel, [((count, width), wide), ((layers, count, columns), wide)], classes, table, ada
    )


def condition_back_kernel(*refs):
    cond, ada = refs[:2]
    grads, (ada_out, silu_out) = refs[2:-2], refs[-2:]
    cond_low = silu_of(cond[...]).astype(low)
    total = jnp.zeros(cond.shape, wide)
    for layer, grad in enumerate(grads):
        ada_out[layer] = contract_rows(cond_low, grad[...])
        total = total + contract_last(grad[...], ada[layer])
    silu_out[...] = total


def condition_back(cond, ada, grads):
    return call(condition_back_kernel, [(ada.shape, wide), (cond.shape, wide)], cond, ada, *grads)


def table_kernel(classes, cond, grad, out):
    value = cond[...]
    gate = 1.0 / (1.0 + jnp.exp(-value))
    slope = gate * (1.0 + value * (1.0 - gate))
    count = out.shape[0]
    hits = (classes[...] == lax.broadcasted_iota(jnp.int32, (count, classes.shape[1]), 0)).astype(wide)
    out[...] = jnp.dot(hits, grad[...] * slope, precision=lax.Precision.HIGHEST, preferred_element_type=wide)


def table_back(classes, cond, grad, count):
    return call(table_kernel, [((count, cond.shape[1]), wide)], classes, cond, grad)[0]


def gradient_blocks_kernel(order, *refs):
    out = refs[-1]
    rest = refs[:-1]
    count, _, span = out.shape
    block = 256
    first = 0
    for factor, own, other in [rest[i : i + 3] for i in range(0, len(rest), 3)]:
        rows = own.shape[0]
        base = first

        @pl.loop(0, factor.shape[1] // block)
        def _(index):
            at = pl.ds(pl.multiple_of(index * block, block), block)
            put = pl.ds(pl.multiple_of(base + index * block, block), block)
            turned = factor[:, at].T
            half = own.shape[1] // 2
            for side in range(2):
                columns = slice(side * half, (side + 1) * half)
                product = (matmul(turned[:, :rows], own[:, columns]) + matmul(turned[:, rows:], other[:, columns])).astype(low)
                for index_in in range(count // 2):
                    place = side * (count // 2) + index_in
                    out[order[place], put, :] = product[:, index_in * span : (index_in + 1) * span]

        first += factor.shape[1]


def gradient_blocks(order, *pairs):
    height = sum(left.shape[1] for left, _ in pairs)
    width = pairs[0][1][0].shape[1]
    count = order.shape[0]
    operands = [value for left, sides in pairs for value in (left, *sides)]
    if not paired(count):
        whole = [contract_rows(left, jnp.concatenate(sides, axis=0)) for left, sides in pairs]
        whole = jnp.concatenate(whole, axis=0).reshape(height, count, width // count)
        return jnp.swapaxes(whole, 0, 1).astype(low)
    return call(gradient_blocks_kernel, [((count, height, width // count), low)], order, *operands, scalars=1)[0]


def gradients(*pairs):
    pairs = [(left if isinstance(left, tuple) else (left, 0, left.shape[1]), sides) for left, sides in pairs]
    spans = [(first, last) for (_, first, last), _ in pairs]
    height = sum(last - first for first, last in spans)
    half = pairs[0][1][0].shape[1] // 2
    operands = [value for (left, _, _), sides in pairs for value in (left, *sides)]
    return call(
        functools.partial(gradient_kernel, spans=spans), [((height, half), low), ((height, half), low)], *operands
    )


def on_device(
    tokens,
    out_grad,
    dest,
    lengths,
    classes,
    class_table,
    w_ada,
    w_qkv,
    head_scale,
    w_proj,
    w_fc1,
    w_fc2,
):
    rows, width = tokens.shape
    groups, shards = lax.axis_size("dp"), lax.axis_size("shard")
    layers = w_ada.shape[0]
    pack = rows * shards
    heads_here = head_scale.shape[1]
    items = lengths.shape[1]
    slots = rows // groups
    columns = w_ada.shape[2]
    me = lax.axis_index("shard")

    near = paired(groups)
    depth, span = w_qkv.shape[1], w_qkv.shape[3]
    flat = [w_qkv[layer].reshape(depth, -1) for layer in range(layers)]
    order = own_order(groups)
    def along(block):
        return lax.all_gather(block, "dp", axis=0, tiled=True, axis_index_groups=slow_groups)

    def ring(block, marker=None):
        block = block if marker is None else tie(block, marker)
        return lax.ppermute(block, "dp", [(i, (i + 2) % 8) for i in range(8)])

    def whole(own, hops, there, other, first, parts):
        size = own.shape[0]
        sources = [(0, 0), (1, 0), (2, 0), (3, 0), (4, first)] + [(5, i * size) for i in range(3)]
        return join([own, *hops, other, there], sources, parts)

    mix_parts = [(depth, 3 * span // 128, 0), (w_proj.shape[1], 1, 1)]
    fc1_parts = [(depth, w_fc1.shape[2] // 128, 0)]
    fc2_parts = [(w_fc2.shape[1], 1, 1)]
    if near:
        mix_a = along(pack_mix(flat[0], w_proj, 0))
        fc1_a, mix_c, fc1_d, fc2_e = (
            along(block) for block in (pack_fc1(w_fc1, 0), pack_mix(flat[1], w_proj, 1), pack_fc1(w_fc1, 1), w_fc2[1])
        )

    def gather_classes(known):
        for offset in (1, 2, 4):
            known = jnp.concatenate([known, swap(known, "dp", offset)], axis=0)
        return known

    if near:
        known = gather_classes(classes)
        index = jnp.arange(groups, dtype=jnp.int32)
        found = (index[:, None] ^ index[None, :]) == lax.axis_index("dp")
        known = jnp.sum(jnp.where(found[:, :, None], known[None], 0), axis=1)
    else:
        known = lax.all_gather(classes, "dp", axis=0, tiled=True)
    all_classes = known.reshape(-1)
    to_slots, to_rows = route(dest, rows)
    leaving = [matmul(to_slots, value).astype(low).reshape(groups, slots, width) for value in (tokens, out_grad)]
    arrived = exchange(jnp.where(all_classes[0] >= 0, jnp.concatenate(leaving, axis=1), 0), groups)

    def sum_pack(part):
        part = part + swap(part, "shard", 1)
        return part + swap(part, "shard", 2)

    cond, part = condition(all_classes[:, None], class_table, w_ada)
    part = sum_pack(part)
    if near:
        there_m = swap(tie(mix_a, part), "dp", 1)
    part = jnp.swapaxes(part.reshape(layers, groups, items, columns), 0, 1)
    upper = lax.reduce_precision(part, 8, 7)
    halves = jnp.stack([upper.astype(low), (part - upper).astype(low)], axis=1)
    halves = exchange(halves.reshape(groups, 2 * layers * items, columns), groups)
    packed = unpack(to_rows, arrived[:, :slots].reshape(rows, width), order)
    carried = jnp.concatenate([packed, swap(packed, "shard", 2)], axis=0).astype(wide)
    grad_packed = unpack(to_rows, arrived[:, slots:].reshape(rows, width), order)
    modulation = spread(halves, order, layers, items, width)
    if near:
        own_b = tie(w_fc2[0], modulation)
        hops_b = straight(own_b)
        other_b = swap(own_b, "dp", 1)
    def across_cores(value):
        return swap(value, "shard", 1)

    def sum_pack_rows(part_own, parts_other, *meanwhile):
        here = gather_cores(part_own, parts_other)
        there = swap(here, "shard", 2)
        return here, there

    place = jnp.concatenate(
        [(me ^ offset) * rows + jnp.arange(rows, dtype=jnp.int32) for offset in (0, 2, 1, 3)]
    )
    member, level = pack_layout(lengths[0], place)
    layout = (member[:, None], level[:, None], member[None, :], level[None, :])
    here_member = member[: 2 * rows, None]
    choose = (jnp.arange(16, dtype=jnp.int32)[:, None] == member[None, : 2 * rows]).astype(low)
    scales = [head_scale[layer][None, :] for layer in range(layers)]
    mods = [modulation[layer] for layer in range(layers)]

    weights = [None] * layers
    saved = []
    first_low = enter(carried, mods[0], here_member, 2, 4)
    for layer in range(layers):
        if not near:
            qkv_full = lax.all_gather(flat[layer], "dp", axis=0, tiled=True)
            proj_full = lax.all_gather(w_proj[layer], "dp", axis=1, tiled=True)
            fc1_full = lax.all_gather(w_fc1[layer], "dp", axis=0, tiled=True)
            fc2_full = lax.all_gather(w_fc2[layer], "dp", axis=1, tiled=True)
        if near and layer == 0:
            there_a = swap(tie(fc1_a, first_low), "dp", 1)
        elif near:
            there_d = swap(tie(fc1_d, first_low), "dp", 1)
        first = (first_low, across_cores(first_low))
        if near:
            mix, mix_there = (mix_c, there_c) if layer else (mix_a, there_m)
            qkv_full, proj_full = join_pair(mix, tie(mix_there, first_low), order, mix_parts)
        part_own, part_a, part_b, *kept = attend(
            *first, qkv_full, proj_full, scales[layer], layout, heads_here
        )
        if near and layer == 0:
            part_a = tie(part_a, *hops_b, other_b)
            there_b = swap(tie(stack(hops_b), part_a), "dp", 1)
        elif near:
            there_e = swap(tie(fc2_e, part_a), "dp", 1)
        if layer == 1:
            part_a = tie(part_a, grad_there)
        here, there = sum_pack_rows(part_own, (part_a, part_b))
        if near:
            there = tie(there, there_d if layer else there_a)
        attended = (here, there)
        middle, second_low = step(carried, *attended, mods[layer], mods[layer], here_member, 0, 3, 5)
        second = (second_low, across_cores(second_low))
        if near:
            fc1, fc1_there = (fc1_d, there_d) if layer else (fc1_a, there_a)
            (fc1_full,) = join_pair(fc1, tie(fc1_there, second_low), order, fc1_parts)
            if layer == 0:
                (fc2_full,) = whole(own_b, hops_b, tie(there_b, second_low), other_b, 0, fc2_parts)
            else:
                (fc2_full,) = join_pair(fc2_e, tie(there_e, second_low), order, fc2_parts)
        weights[layer] = (qkv_full, proj_full, fc1_full, fc2_full)
        part_own, part_a, part_b, slope, activated = mlp(*second, fc1_full, fc2_full)
        if near and layer == 0:
            there_c = swap(tie(mix_c, part_a), "dp", 1)
        branch = sum_pack_rows(part_own, (part_a, part_b))
        saved.append((carried, middle, first, kept, attended, second, slope, activated, branch))
        if layer + 1 < layers:
            grad_there = swap(tie(grad_packed, branch[1]), "shard", 2)
            carried, first_low = step(middle, *branch, mods[layer], mods[layer + 1], here_member, 1, 2, 4)
        else:
            carried = leave(middle, *branch, mods[layer], here_member, 1)
    grad_carried = jnp.concatenate([grad_packed, grad_there], axis=0).astype(wide)

    mixed_out = repack(to_rows, carried, order).reshape(groups, slots, width)

    def give(layer):
        sums = collect(mod_sums[layer], width)
        return unspread(sums, swap(sums, "shard", 1), order, items, columns)

    layer_sums = [None] * layers
    scale_grads = [None] * layers
    mod_sums = [[None] * 6 for _ in range(layers)]
    grad_low, sums = first_back(grad_carried, *saved[-1][-1], mods[-1], here_member, choose, 1)
    mod_sums[-1][1] = (sums, 0)
    for layer in range(layers - 1, -1, -1):
        qkv_full, proj_full, fc1_full, fc2_full = weights[layer]
        carried_in, middle, first, kept, attended, second, slope, activated, branch = saved[layer]
        other = across_cores(grad_low)
        if near and layer == 0:
            other = tie(other, layer_sums[1][1].arrived)
            other = layer_sums[1][1].fold(True, other)
        grad_branch = (grad_low, other)
        if near:
            terms = gradients((activated, grad_branch))
            sums_fc2 = Sums(*terms)
            slope = tie(slope, *terms)
        part_own, part_a, part_b, grad_hidden = mlp_back(*grad_branch, slope, fc1_full, fc2_full)
        if near and layer == 0:
            part_a = tie(part_a, layer_sums[1][0].arrived)
            part_a = layer_sums[1][0].fold(True, part_a)
        here, there = sum_pack_rows(part_own, (part_a, part_b))
        if near:
            terms = gradients((tie(grad_hidden, here), second))
            sums_fc1 = Sums(*terms)
            there = tie(there, *terms, *([layer_sums[1][2].blocks] if layer == 0 else [mixed_out]))
        else:
            sums_fc2 = WholeSums(gradient_blocks(order, (activated, grad_branch)))
            sums_fc1 = WholeSums(gradient_blocks(order, (grad_hidden, second)))
        grad_middle, grad_low, sums = step_back(
            middle, here, there, grad_carried, mods[layer], here_member, choose, 3, (mods[layer], 0, *attended)
        )
        mod_sums[layer][3], mod_sums[layer][5], mod_sums[layer][0] = ((sums, i * width) for i in range(3))
        other = across_cores(grad_low)
        if near and layer == 0:
            other = tie(other, sums_fc2.arrived, layer_sums[1][1].blocks)
            other = sums_fc2.fold(True, other)
        grad_attended = (grad_low, other)
        part_own, part_a, part_b, grad_projected, scale_grads[layer] = attend_back(
            *grad_attended, kept, qkv_full, proj_full, scales[layer], layout, heads_here
        )
        if near and layer == 0:
            terms = gradients(((kept[0], 3 * span, 4 * span), grad_attended), (grad_projected, first))
            part_a = tie(part_a, *terms)
        elif near:
            part_a = tie(part_a, sums_fc2.arrived)
            part_a = sums_fc2.fold(True, part_a)
        here, there = sum_pack_rows(part_own, (part_a, part_b))
        if near:
            if layer > 0:
                terms = gradients(((tie(kept[0], here), 3 * span, 4 * span), grad_attended), (grad_projected, first))
            there = tie(there, *terms)
            if layer == 0:
                there = tie(there, sums_fc1.arrived, layer_sums[1][0].blocks)
                there = sums_fc1.fold(True, there)
            sums_attn = Sums(*terms)
        else:
            sums_attn = WholeSums(gradient_blocks(order, (kept[0][:, 3 * span :], grad_attended), (grad_projected, first)))
        if layer > 0:
            grad_carried, grad_low, sums = step_back(
                carried_in, here, there, grad_middle, mods[layer], here_member, choose, 2, (mods[layer - 1], 1, *saved[layer - 1][-1])
            )
            mod_sums[layer - 1][1] = (sums, 2 * width)
        else:
            grad_carried, sums = step_back(carried_in, here, there, grad_middle, mods[layer], here_member, choose, 2)
        mod_sums[layer][2], mod_sums[layer][4] = (sums, 0), (sums, width)
        layer_sums[layer] = (sums_attn, sums_fc1, sums_fc2)
    if near:
        grad_carried = tie(grad_carried, layer_sums[0][0].arrived)
        layer_sums[0][0].fold(False, grad_carried)

    grads_back = repack(to_rows, grad_carried, order).reshape(groups, slots, width)
    sent = jnp.stack([give(layer) for layer in range(layers)], axis=1).reshape(groups, layers * items * columns)
    if sent.shape[1] % width:
        back = exchange(jnp.concatenate([mixed_out, grads_back], axis=1), groups)
        mods_back = exchange(sent, groups)
    else:
        sent = sent.reshape(groups, -1, width)
        back = exchange(jnp.concatenate([mixed_out, grads_back, sent], axis=1), groups)
        mods_back = back[:, 2 * slots :]
    mixed_back, grads_back = back[:, :slots], back[:, slots : 2 * slots]
    mods_back = mods_back.reshape(groups, layers, items, columns)
    mods_back = [mods_back[:, layer] for layer in range(layers)]

    mixed = contract_rows(to_slots, mixed_back.reshape(rows, width)).astype(low)
    tokens_grad = contract_rows(to_slots, grads_back.reshape(rows, width)).astype(low)
    ada_grad, grad_silu = condition_back(
        cond, w_ada, [back.reshape(groups * items, columns) for back in mods_back]
    )
    logs = jnp.pad(jnp.stack(scale_grads).reshape(1, -1), ((0, 7), (0, cond.shape[1] - layers * heads_here)))
    summed = jnp.concatenate([grad_silu, logs], axis=0)
    if paired(groups):
        for offset in (1, 2, 4):
            summed = summed + swap(summed, "dp", offset)
    else:
        summed = lax.psum(summed, "dp")
    grad_silu = summed[: cond.shape[0]]
    scale_grad = summed[cond.shape[0], : layers * heads_here].reshape(layers, heads_here)
    table_grad = table_back(all_classes[None, :], cond, grad_silu, class_table.shape[0])
    spanned = w_proj.shape[1]
    layer_grads = []
    for layer in range(layers):
        attn, fc1, fc2 = (sums.total(scale_grad) for sums in layer_sums[layer])
        layer_grads.append((attn[spanned:].T.reshape(w_qkv.shape[1:]), attn[:spanned], fc1.T, fc2))
    qkv_grad, proj_grad, fc1_grad, fc2_grad = (
        jnp.stack([layer_grads[layer][i] for layer in range(layers)]) for i in range(4)
    )
    return (
        mixed,
        tokens_grad,
        table_grad,
        ada_grad,
        qkv_grad,
        scale_grad,
        proj_grad,
        fc1_grad,
        fc2_grad,
    )


def solution(mesh):
    placed = (
        P(("dp", "shard"), None),
        P(("dp", "shard"), None),
        P(None, "shard", None),
        P("dp", None),
        P("dp", None),
        P(None, "shard"),
        P(None, "shard", "dp"),
        P(None, "dp", None, "shard"),
        P(None, "shard"),
        P(None, "shard", "dp"),
        P(None, "dp", "shard"),
        P(None, "shard", "dp"),
    )
    return jax.shard_map(
        on_device,
        mesh=mesh,
        in_specs=placed,
        out_specs=(
            P(("dp", "shard"), None),
            P(("dp", "shard"), None),
            P(None, "shard"),
            P(None, "shard", "dp"),
            P(None, "dp", None, "shard"),
            P(None, "shard"),
            P(None, "shard", "dp"),
            P(None, "dp", "shard"),
            P(None, "shard", "dp"),
        ),
        check_vma=False,
    )
```

```python
import functools

import jax
import jax.numpy as jnp
from jax import lax
from jax.experimental import pallas as pl
from jax.experimental.pallas import tpu as pltpu
from jax.sharding import PartitionSpec as P

epsilon = 1e-06
level_ends = (1, 5, 14, 30, 55, 91, 155, 255, 424, 680)
wide = jnp.float32
low = jnp.bfloat16
root = 0.7978845608028654
cubic = 0.044715


def matmul(left, right):
    return jnp.dot(left, right, preferred_element_type=wide)


def contract_rows(left, right):
    return lax.dot_general(left, right, (((0,), (0,)), ((), ())), preferred_element_type=wide)


def contract_last(left, right):
    return lax.dot_general(left, right, (((1,), (1,)), ((), ())), preferred_element_type=wide)


def swap(value, axis, offset):
    size = lax.axis_size(axis)
    return lax.ppermute(value, axis, [(i, i ^ offset) for i in range(size)])


def tie(value, *others):
    return lax.optimization_barrier((value, others))[0]


slow_groups = [[0, 2, 4, 6], [1, 3, 5, 7]]


def paired(groups):
    return groups == 8


def own_order(groups):
    here = lax.axis_index("dp")
    if not paired(groups):
        return jnp.arange(groups, dtype=jnp.int32)
    place = jnp.arange(groups, dtype=jnp.int32)
    return (lax.rem(here // 2 + 4 - place % 4, 4) * 2 + (here % 2 ^ place // 4)).astype(jnp.int32)


def straight(block):
    return [lax.ppermute(block, "dp", [(i, (i + 2 * back) % 8) for i in range(8)]) for back in (1, 2, 3)]


def columns_of(piece, out, first):
    depth, width = piece.shape
    for index in range(width // 128):
        out[first + index * depth : first + (index + 1) * depth, :] = piece[:, index * 128 : (index + 1) * 128]


def pack_mix_kernel(qkv, proj, *refs, layer):
    out = refs[-1]
    columns_of(qkv[...], out, 0)
    first = qkv.shape[0] * qkv.shape[1] // 128
    out[first : first + proj.shape[1], :] = proj[layer]
    if len(refs) > 1:
        out[first + proj.shape[1] :, :] = refs[0][layer]


def pack_mix(qkv, proj, layer, *more):
    height = qkv.shape[0] * qkv.shape[1] // 128 + proj.shape[1] + sum(value.shape[1] for value in more)
    return call(functools.partial(pack_mix_kernel, layer=layer), [((height, 128), low)], qkv, proj, *more)[0]


def pack_fc1_kernel(fc1, out, *, layer):
    columns_of(fc1[layer], out, 0)


def pack_fc1(fc1, layer):
    height = fc1.shape[1] * fc1.shape[2] // 128
    return call(functools.partial(pack_fc1_kernel, layer=layer), [((height, 128), low)], fc1)[0]


def pack_pair_kernel(fc1, fc2, out, *, layer):
    columns_of(fc1[layer], out, 0)
    out[fc2.shape[1] :, :] = fc2[layer]


def pack_pair(fc1, fc2, layer):
    return call(functools.partial(pack_pair_kernel, layer=layer), [((2 * fc2.shape[1], 128), low)], fc1, fc2)[0]


def stack_kernel(*refs):
    out = refs[-1]
    size = refs[0].shape[0]
    for index, ref in enumerate(refs[:-1]):
        out[index * size : (index + 1) * size, :] = ref[...]


def stack(blocks):
    size = blocks[0].shape[0]
    return call(stack_kernel, [((size * len(blocks), 128), low)], *blocks)[0]


def put_block(read, place, outs, parts):
    first = 0
    for out, (depth, columns, axis) in zip(outs, parts):
        for index in range(columns):
            piece = read(first, depth)
            first += depth
            if axis == 0:
                out[place * depth : (place + 1) * depth, index * 128 : (index + 1) * 128] = piece
            else:
                out[:, place * 128 : (place + 1) * 128] = piece


def join_kernel(*refs, sources, parts):
    outs = refs[-len(parts) :]
    for place, (ref, base) in enumerate(sources):
        put_block(lambda first, depth: refs[ref][base + first : base + first + depth, :], place, outs, parts)


def pair_kernel(order, here, there, *outs, parts):
    size = here.shape[0] // 4
    for place in range(8):
        base = (order[place] // 2) * size
        blocks = there if place // 4 else here
        put_block(
            lambda first, depth: blocks[pl.ds(pl.multiple_of(base + first, 128), depth), :], place, outs, parts
        )


def join_pair(here, there, order, parts):
    return call(functools.partial(pair_kernel, parts=parts), joined_shapes(8, parts), order, here, there, scalars=1)


def order_kernel(order, blocks, *outs, parts):
    size = blocks.shape[0] // order.shape[0]
    for place in range(order.shape[0]):
        base = order[place] * size
        put_block(
            lambda first, depth: blocks[pl.ds(pl.multiple_of(base + first, 128), depth), :], place, outs, parts
        )


def joined_shapes(count, parts):
    return [((depth, 128 * count) if axis else (depth * count, columns * 128), low) for depth, columns, axis in parts]


def join(arrays, sources, parts):
    return call(
        functools.partial(join_kernel, sources=sources, parts=parts), joined_shapes(len(sources), parts), *arrays
    )


def join_ordered(blocks, order, parts):
    return call(
        functools.partial(order_kernel, parts=parts), joined_shapes(order.shape[0], parts), order, blocks, scalars=1
    )


def unpack_kernel(order, to_rows, arrived, out, kept):
    kept[...] = matmul(to_rows[...], arrived[...]).astype(low)
    span = out.shape[1] // order.shape[0]
    for place in range(order.shape[0]):
        out[:, place * span : (place + 1) * span] = kept[:, pl.ds(pl.multiple_of(order[place] * span, span), span)]


def unpack(to_rows, arrived, order):
    if not paired(order.shape[0]):
        return matmul(to_rows, arrived).astype(low)
    shape = (to_rows.shape[0], arrived.shape[1])
    return call(
        unpack_kernel, [(shape, low)], order, to_rows, arrived, scratch=[pltpu.VMEM(shape, low)], scalars=1
    )[0]


def repack_kernel(order, to_rows, value, out, kept):
    rows, span = out.shape[0], out.shape[1] // order.shape[0]
    for place in range(order.shape[0]):
        at = pl.ds(pl.multiple_of(order[place] * span, span), span)
        kept[:, at] = value[:rows, place * span : (place + 1) * span].astype(low)
    out[...] = contract_rows(to_rows[...], kept[...]).astype(low)


def repack(to_rows, value, order):
    shape = (to_rows.shape[0], value.shape[1])
    if not paired(order.shape[0]):
        return matmul(to_rows.T, value[: shape[0]].astype(low)).astype(low)
    return call(
        repack_kernel, [(shape, low)], order, to_rows, value, scratch=[pltpu.VMEM(shape, low)], scalars=1
    )[0]


def collect_kernel(*refs, offsets):
    out = refs[-1]
    lines, width = out.shape[0], out.shape[1] // 6
    for part, (ref, first) in enumerate(zip(refs[:-1], offsets)):
        out[:, part * width : (part + 1) * width] = ref[:lines, first : first + width]


def collect(parts, width):
    return call(
        functools.partial(collect_kernel, offsets=[first for _, first in parts]),
        [((8, 6 * width), wide)],
        *[value for value, _ in parts],
    )[0]


def unspread_kernel(order, own, other, out):
    count, _, columns = out.shape
    blocks = columns // 128
    for part in range(6):
        for place in range(count):
            first = (part * count + place) * 128
            block = order[place] + part * count
            at = pl.ds(pl.multiple_of(lax.rem(block, blocks) * 128, 128), 128)
            out[block // blocks, :, at] = (own[:, first : first + 128] + other[:, first : first + 128]).astype(low)


def unspread(own, other, order, items, columns):
    count = order.shape[0]
    if paired(count):
        return call(unspread_kernel, [((count, own.shape[0], columns), low)], order, own, other, scalars=1)[0][:, :items]
    return jnp.swapaxes((own + other).astype(low)[:items].reshape(items, count, columns), 0, 1)


def spread_kernel(order, arrived, out):
    count, lines, columns = arrived.shape
    layers, parts, items, _ = out.shape
    blocks = columns // 128
    for part in range(parts):
        for place in range(count):
            block = order[place] + part * count
            source = block // blocks
            at = pl.ds(pl.multiple_of(lax.rem(block, blocks) * 128, 128), 128)
            rows = arrived[source, :, at].astype(wide)
            total = rows[: lines // 2] + rows[lines // 2 :]
            for layer in range(layers):
                out[layer, part, :, place * 128 : (place + 1) * 128] = total[layer * items : (layer + 1) * items]


def spread(arrived, order, layers, items, width):
    count, lines, columns = arrived.shape
    if paired(count):
        return call(spread_kernel, [((layers, 6, items, width), wide)], order, arrived, scalars=1)[0]
    halves = arrived.astype(wide).reshape(count, 2, layers, items, columns)
    whole = jnp.transpose(halves[:, 0] + halves[:, 1], (1, 2, 0, 3)).reshape(layers, items, 6, width)
    return jnp.swapaxes(whole, 1, 2)


def fold_kernel(slow, kept, arrived, out):
    span = out.shape[2]
    for back in range(4):
        columns = slice(back * span, (back + 1) * span)
        out[lax.rem(slow[0] + 4 - back, 4)] = (kept[:, columns].astype(wide) + arrived[:, columns].astype(wide)).astype(low)


def fold(kept, arrived, slow):
    height, half = kept.shape
    return call(fold_kernel, [((4, height, half // 4), low)], slow, kept, arrived, scalars=1)[0]


class Sums:
    def __init__(self, kept, sent):
        self.kept = kept
        self.arrived = swap(sent, "dp", 1)

    def fold(self, along, marker):
        if along:
            slow = (lax.axis_index("dp") // 2).astype(jnp.int32).reshape(1)
            blocks = fold(self.kept, tie(self.arrived, marker), slow)
            self.blocks = lax.psum_scatter(
                blocks, "dp", scatter_dimension=0, axis_index_groups=slow_groups, tiled=True
            )
            return tie(marker, blocks)
        self.blocks = None
        total = self.kept.astype(wide) + tie(self.arrived, marker).astype(wide)
        span = total.shape[1] // 4
        self.parts = [total[:, i * span : (i + 1) * span] for i in range(4)]
        for back in (1, 2, 3):
            pairs = [(i, (i + 8 - 2 * back) % 8) for i in range(8)]
            self.parts[back] = lax.ppermute(self.parts[back].astype(low), "dp", pairs)

    def total(self, marker):
        if self.blocks is not None:
            return tie(self.blocks, marker).reshape(self.blocks.shape[1:]).astype(wide)
        parts = [tie(part, marker) for part in self.parts]
        return parts[0] + parts[1].astype(wide) + parts[2].astype(wide) + parts[3].astype(wide)


class WholeSums:
    def __init__(self, blocks):
        self.arrived = blocks
        self.result = lax.psum_scatter(blocks, "dp", scatter_dimension=0, tiled=True)

    def fold(self):
        pass

    def total(self, marker):
        return tie(self.result, marker).reshape(self.result.shape[1:]).astype(wide)


def gather_cores_kernel(own, first, second, out):
    half = first.shape[0]
    out[:half, :] = (own[:half, :] + first[...].astype(wide)).astype(low)
    out[half:, :] = (own[half:, :] + second[...].astype(wide)).astype(low)


def gather_cores(part_own, parts_other):
    arrived = [swap(part, "shard", 1) for part in parts_other]
    return call(gather_cores_kernel, [(part_own.shape, low)], part_own, *arrived)[0]


def route(dest, rows):
    table = dest[:, 0, :]
    groups = table.shape[0]
    capacity = rows // groups
    here = lax.axis_index("dp")
    own = lax.dynamic_index_in_dim(table, here, 0, keepdims=False)
    pack = own // rows
    index = jnp.arange(rows, dtype=jnp.int32)
    earlier = index[None, :] < index[:, None]
    rank = jnp.sum((earlier & (pack[None, :] == pack[:, None])).astype(jnp.int32), axis=1)
    slot = pack * capacity + rank
    to_slots = (slot[None, :] == index[:, None]).astype(low)
    mine = table // rows == here
    rank_in = jnp.sum((earlier[None] & mine[:, None, :]).astype(jnp.int32), axis=2)
    slot_in = jnp.arange(groups, dtype=jnp.int32)[:, None] * capacity + rank_in
    slot_in = jnp.where(mine, slot_in, rows).reshape(-1)
    row_in = (table % rows).reshape(-1)
    by_row = (row_in[None, :] == index[:, None]).astype(low)
    by_slot = (slot_in[None, :] == index[:, None]).astype(low)
    to_rows = contract_last(by_row, by_slot).astype(low)
    return to_slots, to_rows


def exchange(value, groups):
    return lax.all_to_all(value, "dp", split_axis=0, concat_axis=0, tiled=True)


def pack_layout(lengths, place):
    ends = jnp.cumsum(lengths)
    starts = ends - lengths
    member = jnp.sum((place[:, None] >= ends[None, :]).astype(jnp.int32), axis=1)
    onehot = member[:, None] == jnp.arange(lengths.shape[0], dtype=jnp.int32)[None, :]
    start = jnp.sum(jnp.where(onehot, starts[None, :], jnp.int32(0)), axis=1)
    bounds = jnp.array(level_ends, dtype=jnp.int32)
    level = jnp.sum(((place - start)[:, None] >= bounds[None, :]).astype(jnp.int32), axis=1)
    return member, level


grant = 24
stripe = 64


def call(kernel, outs, *operands, scratch=(), scalars=0, cost=400_000_000):
    spec = pl.BlockSpec(memory_space=pltpu.VMEM)
    return pl.pallas_call(
        kernel,
        out_shape=[jax.ShapeDtypeStruct(shape, kind) for shape, kind in outs],
        in_specs=[pl.BlockSpec(memory_space=pltpu.SMEM)] * scalars + [spec] * (len(operands) - scalars),
        out_specs=[spec] * len(outs),
        scratch_shapes=list(scratch),
        cost_estimate=pl.CostEstimate(flops=cost, bytes_accessed=1, transcendentals=0),
        compiler_params=pltpu.CompilerParams(vmem_limit_bytes=grant << 20),
    )(*operands)


def pick(member, table):
    items = table.shape[0]
    result = table[items - 1 : items, :]
    for item in range(items - 2, -1, -1):
        result = jnp.where(member == item, table[item : item + 1, :], result)
    return result


def normed(value):
    centered = value - jnp.mean(value, axis=-1, keepdims=True)
    inverse = lax.rsqrt(jnp.mean(centered * centered, axis=-1, keepdims=True) + epsilon)
    return centered * inverse, inverse


def stripes(rows, body):
    @pl.loop(0, rows // stripe)
    def _(index):
        first = pl.multiple_of(index * stripe, stripe)
        body(pl.ds(first, stripe), pl.ds(pl.multiple_of(lax.rem(first + rows // 2, rows), stripe), stripe))


def enter_kernel(value, mods, member, out, *, scale, shift):
    def body(at, _):
        who = member[at, :]
        unit, _inverse = normed(value[at, :])
        out[at, :] = (unit * (1.0 + pick(who, mods[scale])) + pick(who, mods[shift])).astype(low)

    stripes(value.shape[0], body)


def enter(value, mods, member, scale, shift):
    return call(
        functools.partial(enter_kernel, scale=scale, shift=shift), [(value.shape, low)], value, mods, member
    )[0]


def step_kernel(value, here, there, mods_gain, mods, member, out, low_out, *, gain, scale, shift):
    def body(at, across):
        who = member[at, :]
        branch = here[at, :].astype(wide) + there[across, :].astype(wide)
        total = value[at, :] + pick(who, mods_gain[gain]) * branch
        out[at, :] = total
        unit, _inverse = normed(total)
        low_out[at, :] = (unit * (1.0 + pick(who, mods[scale])) + pick(who, mods[shift])).astype(low)

    stripes(value.shape[0], body)


def step(value, here, there, mods_gain, mods, member, gain, scale, shift):
    return call(
        functools.partial(step_kernel, gain=gain, scale=scale, shift=shift),
        [(value.shape, wide), (value.shape, low)],
        value, here, there, mods_gain, mods, member,
    )


def leave_kernel(value, here, there, mods, member, out, *, gain):
    def body(at, across):
        branch = here[at, :].astype(wide) + there[across, :].astype(wide)
        out[at, :] = value[at, :] + pick(member[at, :], mods[gain]) * branch

    stripes(value.shape[0], body)


def leave(value, here, there, mods, member, gain):
    return call(
        functools.partial(leave_kernel, gain=gain), [(value.shape, wide)], value, here, there, mods, member
    )[0]


def put_part(targets, at, value):
    if len(targets) == 1:
        targets[0][at, :] = value.astype(targets[0].dtype)
        return
    half = targets[0].shape[0]
    for index, target in enumerate(targets):
        first, last = max(at.start, index * half), min(at.stop, (index + 1) * half)
        if first < last:
            target[first - index * half : last - index * half, :] = value[first - at.start : last - at.start].astype(target.dtype)


def mlp_kernel(own, other, fc1, fc2, part_own, part_a, part_b, slope_out, act_out):
    half = own.shape[0]
    for place, source, target in ((0, own, (part_own,)), (1, other, (part_a, part_b))):
        for index in range(half // 256):
            at = slice(index * 256, (index + 1) * 256)
            put = slice(place * half + index * 256, place * half + (index + 1) * 256)
            hidden = matmul(source[at, :], fc1[...])
            square = hidden * hidden
            bent = jnp.tanh(hidden * (root + (root * cubic) * square))
            share = 0.5 + 0.5 * bent
            activated = (hidden * share).astype(low)
            slope = share + (hidden * (1.0 - bent * bent)) * (0.5 * root + (1.5 * root * cubic) * square)
            slope_out[put, :] = slope.astype(low)
            act_out[put, :] = activated
            put_part(target, at, matmul(activated, fc2[...]))


def mlp(own, other, fc1, fc2):
    half, width = own.shape
    units = fc1.shape[1]
    return call(
        mlp_kernel,
        [((half, width), wide), ((half // 2, width), low), ((half // 2, width), low), ((2 * half, units), low), ((2 * half, units), low)],
        own, other, fc1, fc2,
    )


def mlp_back_kernel(own, other, slope, fc1, fc2, part_own, part_a, part_b, grad_out):
    half = own.shape[0]
    for place, source, target in ((0, own, (part_own,)), (1, other, (part_a, part_b))):
        for index in range(half // 256):
            at = slice(index * 256, (index + 1) * 256)
            put = slice(place * half + index * 256, place * half + (index + 1) * 256)
            grad_activated = contract_last(source[at, :], fc2[...])
            grad_hidden = (grad_activated * slope[put, :].astype(wide)).astype(low)
            grad_out[put, :] = grad_hidden
            put_part(target, at, contract_last(grad_hidden, fc1[...]))


def mlp_back(own, other, slope, fc1, fc2):
    half, width = own.shape
    return call(
        mlp_back_kernel,
        [((half, width), wide), ((half // 2, width), low), ((half // 2, width), low), (slope.shape, low)],
        own, other, slope, fc1, fc2,
    )


def heads_of(shape, heads):
    lane = lax.broadcasted_iota(jnp.int32, shape, 1)
    span = shape[1] // heads
    return [(lane >= head * span) & (lane < (head + 1) * span) for head in range(heads)]


def head_sums(value, masks):
    return [jnp.sum(jnp.where(mask, value, 0.0), axis=1, keepdims=True) for mask in masks]


def by_head(columns, masks):
    result = columns[-1]
    for column, mask in zip(columns[-2::-1], masks[-2::-1]):
        result = jnp.where(mask, column, result)
    return result


def allowed_at(member, level, member_row, level_row, at):
    return (member[at, :] == member_row[...]) & (level_row[...] <= level[at, :])


def attend_kernel(
    own, other, qkv, proj, scale, member, level, member_row, level_row,
    part_own, part_a, part_b, kept, inverse_out, *, heads,
):
    half = own.shape[0]
    span = qkv.shape[1] // 3
    block = 256
    queries, keys, values, heads_out = (kept.at[:, i * span : (i + 1) * span] for i in range(4))
    for place, source in ((0, own), (1, other)):
        @pl.loop(0, half // block)
        def _(index):
            at = pl.ds(pl.multiple_of(index * block, block), block)
            put = pl.ds(pl.multiple_of(place * half + index * block, block), block)
            projected = matmul(source[at, :], qkv[...])
            masks = heads_of((block, span), heads)
            query, key = projected[:, :span], projected[:, span : 2 * span]
            inverse_q = [lax.rsqrt(total + epsilon) for total in head_sums(query * query, masks)]
            inverse_k = [lax.rsqrt(total + epsilon) for total in head_sums(key * key, masks)]
            rises = [jnp.exp(scale[:, head : head + 1]) for head in range(heads)]
            queries[put, :] = (query * by_head([i * a for i, a in zip(inverse_q, rises)], masks)).astype(low)
            keys[put, :] = (key * by_head(inverse_k, masks)).astype(low)
            values[put, :] = projected[:, 2 * span :].astype(low)
            inverse_out[put, : 2 * heads] = jnp.concatenate(inverse_q + inverse_k, axis=1)

    rows = 2 * half
    for place, target in ((0, (part_own,)), (1, (part_a, part_b))):
        for index in range(half // block):
            at = slice(index * block, (index + 1) * block)
            put = slice(place * half + index * block, place * half + (index + 1) * block)
            allowed = allowed_at(member, level, member_row, level_row, put)
            query = queries[put, :]
            masks = heads_of((block, span), heads)
            wide_masks = heads_of((rows, span), heads)
            outputs = jnp.zeros((block, span), wide)
            inverses = []
            for head in range(heads):
                scores = contract_last(jnp.where(masks[head], query, jnp.zeros_like(query)), keys[...])
                raised = jnp.where(allowed, jnp.exp(scores - jnp.exp(scale[:, head : head + 1])), 0.0)
                inverse = 1.0 / jnp.sum(raised, axis=1, keepdims=True)
                inverses.append(inverse)
                weights = (raised * inverse).astype(low)
                outputs = outputs + matmul(weights, jnp.where(wide_masks[head], values[...], jnp.zeros((), low)))
            inverse_out[put, 2 * heads :] = jnp.concatenate(inverses, axis=1)
            outputs = outputs.astype(low)
            heads_out[put, :] = outputs
            put_part(target, at, matmul(outputs, proj[...]))


def attend(own, other, qkv, proj, scale, layout, heads):
    half, width = own.shape
    rows, span = 2 * half, qkv.shape[1] // 3
    return call(
        functools.partial(attend_kernel, heads=heads),
        [((half, width), wide), ((half // 2, width), low), ((half // 2, width), low)] + [((rows, 4 * span), low), ((rows, 3 * heads), wide)],
        own, other, qkv, proj, scale, *layout,
    )


def attend_back_kernel(
    own, other, kept, inverse_in, qkv, proj, scale, member, level, member_row, level_row,
    part_own, part_a, part_b, grad_out, log_out,
    grads, grad_queries, key_sums_t, value_sums_t, *, heads,
):
    half = own.shape[0]
    rows = 2 * half
    span = qkv.shape[1] // 3
    block = 256
    queries, keys, values = (kept.at[:, i * span : (i + 1) * span] for i in range(3))
    grads[:half, :] = contract_last(own[...], proj[...]).astype(low)
    grads[half:, :] = contract_last(other[...], proj[...]).astype(low)
    key_sums_t[...] = jnp.zeros_like(key_sums_t)
    value_sums_t[...] = jnp.zeros_like(value_sums_t)
    deep = span // heads
    step_rows = 256

    @pl.loop(0, rows // step_rows)
    def _(index):
        put = pl.ds(pl.multiple_of(index * step_rows, step_rows), step_rows)
        allowed = allowed_at(member, level, member_row, level_row, put)
        query, grad = queries[put, :], grads[put, :]
        query_t, grad_t = query.astype(wide).T.astype(low), grad.astype(wide).T.astype(low)
        masks = heads_of((step_rows, span), heads)
        wide_masks = heads_of((rows, span), heads)
        outputs = jnp.zeros((step_rows, span), wide)
        for head in range(heads):
            scores = contract_last(jnp.where(masks[head], query, jnp.zeros_like(query)), keys[...])
            raised = jnp.where(allowed, jnp.exp(scores - jnp.exp(scale[:, head : head + 1])), 0.0)
            weights = raised * inverse_in[put, 2 * heads + head : 2 * heads + head + 1]
            grad_weights = contract_last(jnp.where(masks[head], grad, jnp.zeros_like(grad)), values[...])
            inner = jnp.sum(weights * grad_weights, axis=1, keepdims=True)
            grad_scores = (weights * (grad_weights - inner)).astype(low)
            outputs = outputs + matmul(grad_scores, jnp.where(wide_masks[head], keys[...], jnp.zeros((), low)))
            these = slice(head * deep, (head + 1) * deep)
            key_sums_t[these, :] += matmul(query_t[these, :], grad_scores)
            value_sums_t[these, :] += matmul(grad_t[these, :], weights.astype(low))
        grad_queries[put, :] = outputs

    log_out[...] = jnp.zeros_like(log_out)
    grad_keys = key_sums_t[...].T
    grad_out[:, 2 * span :] = value_sums_t[...].T.astype(low)
    rises = [jnp.exp(scale[:, head : head + 1]) for head in range(heads)]
    for place, target in ((0, (part_own,)), (1, (part_a, part_b))):
        for index in range(half // block):
            put = slice(place * half + index * block, place * half + (index + 1) * block)
            at = slice(index * block, (index + 1) * block)
            masks = heads_of((block, span), heads)
            query, key = queries[put, :].astype(wide), keys[put, :].astype(wide)
            grad_query, grad_key = grad_queries[put, :], grad_keys[put, :]
            inverse = [inverse_in[put, i : i + 1] for i in range(2 * heads)]
            dots_q, dots_k = head_sums(query * grad_query, masks), head_sums(key * grad_key, masks)
            log_out[...] += jnp.concatenate([jnp.sum(x, axis=0, keepdims=True) for x in dots_q], axis=1)
            first = by_head([a * i for a, i in zip(rises, inverse[:heads])], masks)
            second = by_head([d * i / a for a, d, i in zip(rises, dots_q, inverse[:heads])], masks)
            grad_out[put, :span] = (grad_query * first - query * second).astype(low)
            first = by_head(inverse[heads:], masks)
            second = by_head([d * i for d, i in zip(dots_k, inverse[heads:])], masks)
            grad_out[put, span : 2 * span] = (grad_key * first - key * second).astype(low)
            put_part(target, at, contract_last(grad_out[put, :], qkv[...]))


def attend_back(own, other, kept, qkv, proj, scale, layout, heads):
    half, width = own.shape
    rows, span = 2 * half, qkv.shape[1] // 3
    return call(
        functools.partial(attend_back_kernel, heads=heads),
        [((half, width), wide), ((half // 2, width), low), ((half // 2, width), low), ((rows, 3 * span), low), ((1, heads), wide)],
        own, other, *kept, qkv, proj, scale, *layout,
        scratch=[pltpu.VMEM((rows, span), low), pltpu.VMEM((rows, span), wide)]
        + [pltpu.VMEM((span, rows), wide), pltpu.VMEM((span, rows), wide)],
    )


def step_back_kernel(
    value, here, there, grad, mods, mods_gain, branch_here, branch_there, member, choose,
    grad_out, low_out, sums_out, terms, *, scale, gain,
):
    width = value.shape[1]

    def body(at, across):
        who = member[at, :]
        unit, inverse = normed(value[at, :])
        arrived = here[at, :].astype(wide) + there[across, :].astype(wide)
        scaled = arrived * (1.0 + pick(who, mods[scale]))
        total = grad[at, :] + inverse * (
            scaled
            - jnp.mean(scaled, axis=-1, keepdims=True)
            - unit * jnp.mean(scaled * unit, axis=-1, keepdims=True)
        )
        grad_out[at, :] = total
        terms[at, : width] = (arrived * unit).astype(low)
        terms[at, width : 2 * width] = arrived.astype(low)
        if gain is not None:
            branch = branch_here[at, :].astype(wide) + branch_there[across, :].astype(wide)
            terms[at, 2 * width :] = (total * branch).astype(low)
            low_out[at, :] = (total * pick(who, mods_gain[gain])).astype(low)

    stripes(value.shape[0], body)
    sums_out[...] = matmul(choose[...], terms[...])


def last_back_kernel(value, here, there, grad, mods, member, choose, grad_out, sums_out, terms, *, scale):
    step_back_kernel(
        value, here, there, grad, mods, None, None, None, member, choose,
        grad_out, None, sums_out, terms, scale=scale, gain=None,
    )


def step_back(value, here, there, grad, mods, member, choose, scale, before=None):
    rows, width = value.shape
    lines = choose.shape[0]
    if before is None:
        return call(
            functools.partial(last_back_kernel, scale=scale),
            [((rows, width), wide), ((lines, 2 * width), wide)],
            value, here, there, grad, mods, member, choose,
            scratch=[pltpu.VMEM((rows, 2 * width), low)],
        )
    mods_gain, gain, branch_here, branch_there = before
    return call(
        functools.partial(step_back_kernel, scale=scale, gain=gain),
        [((rows, width), wide), ((rows, width), low), ((lines, 3 * width), wide)],
        value, here, there, grad, mods, mods_gain, branch_here, branch_there, member, choose,
        scratch=[pltpu.VMEM((rows, 3 * width), low)],
    )


def first_back_kernel(grad, here, there, mods, member, choose, low_out, sums_out, terms, *, gain):
    def body(at, across):
        branch = here[at, :].astype(wide) + there[across, :].astype(wide)
        terms[at, :] = (grad[at, :] * branch).astype(low)
        low_out[at, :] = (grad[at, :] * pick(member[at, :], mods[gain])).astype(low)

    stripes(grad.shape[0], body)
    sums_out[...] = matmul(choose[...], terms[...])


def first_back(grad, here, there, mods, member, choose, gain):
    rows, width = grad.shape
    return call(
        functools.partial(first_back_kernel, gain=gain),
        [((rows, width), low), ((choose.shape[0], width), wide)],
        grad, here, there, mods, member, choose,
        scratch=[pltpu.VMEM((rows, width), low)],
    )


def gradient_kernel(*refs, spans):
    kept, sent = refs[-2:]
    rest = refs[:-2]
    half = kept.shape[1]
    first = 0
    for (begin, end), factor, own, other in [(spans[i // 3], *rest[i : i + 3]) for i in range(0, len(rest), 3)]:
        rows = own.shape[0]
        put = slice(first, first + end - begin)
        turned = factor[:, begin:end].T
        kept[put, :] = (matmul(turned[:, :rows], own[:, :half]) + matmul(turned[:, rows:], other[:, :half])).astype(low)
        sent[put, :] = (matmul(turned[:, :rows], own[:, half:]) + matmul(turned[:, rows:], other[:, half:])).astype(low)
        first += end - begin


def silu_of(value):
    return value / (1.0 + jnp.exp(-value))


def condition_kernel(classes, table, ada, cond_out, part_out):
    count = table.shape[0]
    hits = (classes[...] == lax.broadcasted_iota(jnp.int32, (classes.shape[0], count), 1)).astype(low)
    cond = matmul(hits, table[...])
    cond_out[...] = cond
    cond_low = silu_of(cond).astype(low)
    for layer in range(ada.shape[0]):
        part_out[layer] = matmul(cond_low, ada[layer])


def condition(classes, table, ada):
    count, width = classes.shape[0], table.shape[1]
    layers, _, columns = ada.shape
    return call(
        condition_kernel, [((count, width), wide), ((layers, count, columns), wide)], classes, table, ada
    )


def condition_back_kernel(*refs):
    cond, ada = refs[:2]
    grads, (ada_out, silu_out) = refs[2:-2], refs[-2:]
    cond_low = silu_of(cond[...]).astype(low)
    total = jnp.zeros(cond.shape, wide)
    for layer, grad in enumerate(grads):
        ada_out[layer] = contract_rows(cond_low, grad[...])
        total = total + contract_last(grad[...], ada[layer])
    silu_out[...] = total


def condition_back(cond, ada, grads):
    return call(condition_back_kernel, [(ada.shape, wide), (cond.shape, wide)], cond, ada, *grads)


def table_kernel(classes, cond, grad, out):
    value = cond[...]
    gate = 1.0 / (1.0 + jnp.exp(-value))
    slope = gate * (1.0 + value * (1.0 - gate))
    count = out.shape[0]
    hits = (classes[...] == lax.broadcasted_iota(jnp.int32, (count, classes.shape[1]), 0)).astype(wide)
    out[...] = jnp.dot(hits, grad[...] * slope, precision=lax.Precision.HIGHEST, preferred_element_type=wide)


def table_back(classes, cond, grad, count):
    return call(table_kernel, [((count, cond.shape[1]), wide)], classes, cond, grad)[0]


def gradient_blocks_kernel(order, *refs):
    out = refs[-1]
    rest = refs[:-1]
    count, _, span = out.shape
    block = 256
    first = 0
    for factor, own, other in [rest[i : i + 3] for i in range(0, len(rest), 3)]:
        rows = own.shape[0]
        base = first

        @pl.loop(0, factor.shape[1] // block)
        def _(index):
            at = pl.ds(pl.multiple_of(index * block, block), block)
            put = pl.ds(pl.multiple_of(base + index * block, block), block)
            turned = factor[:, at].T
            half = own.shape[1] // 2
            for side in range(2):
                columns = slice(side * half, (side + 1) * half)
                product = (matmul(turned[:, :rows], own[:, columns]) + matmul(turned[:, rows:], other[:, columns])).astype(low)
                for index_in in range(count // 2):
                    place = side * (count // 2) + index_in
                    out[order[place], put, :] = product[:, index_in * span : (index_in + 1) * span]

        first += factor.shape[1]


def gradient_blocks(order, *pairs):
    height = sum(left.shape[1] for left, _ in pairs)
    width = pairs[0][1][0].shape[1]
    count = order.shape[0]
    operands = [value for left, sides in pairs for value in (left, *sides)]
    if not paired(count):
        whole = [contract_rows(left, jnp.concatenate(sides, axis=0)) for left, sides in pairs]
        whole = jnp.concatenate(whole, axis=0).reshape(height, count, width // count)
        return jnp.swapaxes(whole, 0, 1).astype(low)
    return call(gradient_blocks_kernel, [((count, height, width // count), low)], order, *operands, scalars=1)[0]


def gradients(*pairs):
    pairs = [(left if isinstance(left, tuple) else (left, 0, left.shape[1]), sides) for left, sides in pairs]
    spans = [(first, last) for (_, first, last), _ in pairs]
    height = sum(last - first for first, last in spans)
    half = pairs[0][1][0].shape[1] // 2
    operands = [value for (left, _, _), sides in pairs for value in (left, *sides)]
    return call(
        functools.partial(gradient_kernel, spans=spans), [((height, half), low), ((height, half), low)], *operands
    )


def on_device(
    tokens,
    out_grad,
    dest,
    lengths,
    classes,
    class_table,
    w_ada,
    w_qkv,
    head_scale,
    w_proj,
    w_fc1,
    w_fc2,
):
    rows, width = tokens.shape
    groups, shards = lax.axis_size("dp"), lax.axis_size("shard")
    layers = w_ada.shape[0]
    pack = rows * shards
    heads_here = head_scale.shape[1]
    items = lengths.shape[1]
    slots = rows // groups
    columns = w_ada.shape[2]
    me = lax.axis_index("shard")

    near = paired(groups)
    depth, span = w_qkv.shape[1], w_qkv.shape[3]
    flat = [w_qkv[layer].reshape(depth, -1) for layer in range(layers)]
    order = own_order(groups)
    def along(block):
        return lax.all_gather(block, "dp", axis=0, tiled=True, axis_index_groups=slow_groups)

    def ring(block, marker=None):
        block = block if marker is None else tie(block, marker)
        return lax.ppermute(block, "dp", [(i, (i + 2) % 8) for i in range(8)])

    def whole(own, hops, there, other, first, parts):
        size = own.shape[0]
        sources = [(0, 0), (1, 0), (2, 0), (3, 0), (4, first)] + [(5, i * size) for i in range(3)]
        return join([own, *hops, other, there], sources, parts)

    mix_parts = [(depth, 3 * span // 128, 0), (w_proj.shape[1], 1, 1)]
    fc1_parts = [(depth, w_fc1.shape[2] // 128, 0)]
    fc2_parts = [(w_fc2.shape[1], 1, 1)]
    if near:
        mix_a = along(pack_mix(flat[0], w_proj, 0))
        fc1_a, mix_c, fc1_d, fc2_e = (
            along(block) for block in (pack_fc1(w_fc1, 0), pack_mix(flat[1], w_proj, 1), pack_fc1(w_fc1, 1), w_fc2[1])
        )

    def gather_classes(known):
        for offset in (1, 2, 4):
            known = jnp.concatenate([known, swap(known, "dp", offset)], axis=0)
        return known

    if near:
        known = gather_classes(classes)
        index = jnp.arange(groups, dtype=jnp.int32)
        found = (index[:, None] ^ index[None, :]) == lax.axis_index("dp")
        known = jnp.sum(jnp.where(found[:, :, None], known[None], 0), axis=1)
    else:
        known = lax.all_gather(classes, "dp", axis=0, tiled=True)
    all_classes = known.reshape(-1)
    to_slots, to_rows = route(dest, rows)
    leaving = [matmul(to_slots, value).astype(low).reshape(groups, slots, width) for value in (tokens, out_grad)]
    arrived = exchange(jnp.where(all_classes[0] >= 0, jnp.concatenate(leaving, axis=1), 0), groups)

    def sum_pack(part):
        part = part + swap(part, "shard", 1)
        return part + swap(part, "shard", 2)

    cond, part = condition(all_classes[:, None], class_table, w_ada)
    part = sum_pack(part)
    if near:
        there_m = swap(tie(mix_a, part), "dp", 1)
    part = jnp.swapaxes(part.reshape(layers, groups, items, columns), 0, 1)
    upper = lax.reduce_precision(part, 8, 7)
    halves = jnp.stack([upper.astype(low), (part - upper).astype(low)], axis=1)
    halves = exchange(halves.reshape(groups, 2 * layers * items, columns), groups)
    packed = unpack(to_rows, arrived[:, :slots].reshape(rows, width), order)
    carried = jnp.concatenate([packed, swap(packed, "shard", 2)], axis=0).astype(wide)
    grad_packed = unpack(to_rows, arrived[:, slots:].reshape(rows, width), order)
    modulation = spread(halves, order, layers, items, width)
    if near:
        own_b = tie(w_fc2[0], modulation)
        hops_b = straight(own_b)
        other_b = swap(own_b, "dp", 1)
    def across_cores(value):
        return swap(value, "shard", 1)

    def sum_pack_rows(part_own, parts_other, *meanwhile):
        here = gather_cores(part_own, parts_other)
        there = swap(here, "shard", 2)
        return here, there

    place = jnp.concatenate(
        [(me ^ offset) * rows + jnp.arange(rows, dtype=jnp.int32) for offset in (0, 2, 1, 3)]
    )
    member, level = pack_layout(lengths[0], place)
    layout = (member[:, None], level[:, None], member[None, :], level[None, :])
    here_member = member[: 2 * rows, None]
    choose = (jnp.arange(16, dtype=jnp.int32)[:, None] == member[None, : 2 * rows]).astype(low)
    scales = [head_scale[layer][None, :] for layer in range(layers)]
    mods = [modulation[layer] for layer in range(layers)]

    weights = [None] * layers
    saved = []
    first_low = enter(carried, mods[0], here_member, 2, 4)
    for layer in range(layers):
        if not near:
            qkv_full = lax.all_gather(flat[layer], "dp", axis=0, tiled=True)
            proj_full = lax.all_gather(w_proj[layer], "dp", axis=1, tiled=True)
            fc1_full = lax.all_gather(w_fc1[layer], "dp", axis=0, tiled=True)
            fc2_full = lax.all_gather(w_fc2[layer], "dp", axis=1, tiled=True)
        if near and layer == 0:
            there_a = swap(tie(fc1_a, first_low), "dp", 1)
        elif near:
            there_d = swap(tie(fc1_d, first_low), "dp", 1)
        first = (first_low, across_cores(first_low))
        if near:
            mix, mix_there = (mix_c, there_c) if layer else (mix_a, there_m)
            qkv_full, proj_full = join_pair(mix, tie(mix_there, first_low), order, mix_parts)
        part_own, part_a, part_b, *kept = attend(
            *first, qkv_full, proj_full, scales[layer], layout, heads_here
        )
        if near and layer == 0:
            part_a = tie(part_a, *hops_b, other_b)
            there_b = swap(tie(stack(hops_b), part_a), "dp", 1)
        elif near:
            there_e = swap(tie(fc2_e, part_a), "dp", 1)
        if layer == 1:
            part_a = tie(part_a, grad_there)
        here, there = sum_pack_rows(part_own, (part_a, part_b))
        if near:
            there = tie(there, there_d if layer else there_a)
        attended = (here, there)
        middle, second_low = step(carried, *attended, mods[layer], mods[layer], here_member, 0, 3, 5)
        second = (second_low, across_cores(second_low))
        if near:
            fc1, fc1_there = (fc1_d, there_d) if layer else (fc1_a, there_a)
            (fc1_full,) = join_pair(fc1, tie(fc1_there, second_low), order, fc1_parts)
            if layer == 0:
                (fc2_full,) = whole(own_b, hops_b, tie(there_b, second_low), other_b, 0, fc2_parts)
            else:
                (fc2_full,) = join_pair(fc2_e, tie(there_e, second_low), order, fc2_parts)
        weights[layer] = (qkv_full, proj_full, fc1_full, fc2_full)
        part_own, part_a, part_b, slope, activated = mlp(*second, fc1_full, fc2_full)
        if near and layer == 0:
            there_c = swap(tie(mix_c, part_a), "dp", 1)
        branch = sum_pack_rows(part_own, (part_a, part_b))
        saved.append((carried, middle, first, kept, attended, second, slope, activated, branch))
        if layer + 1 < layers:
            grad_there = swap(tie(grad_packed, branch[1]), "shard", 2)
            carried, first_low = step(middle, *branch, mods[layer], mods[layer + 1], here_member, 1, 2, 4)
        else:
            carried = leave(middle, *branch, mods[layer], here_member, 1)
    grad_carried = jnp.concatenate([grad_packed, grad_there], axis=0).astype(wide)

    mixed_out = repack(to_rows, carried, order).reshape(groups, slots, width)

    def give(layer):
        sums = collect(mod_sums[layer], width)
        return unspread(sums, swap(sums, "shard", 1), order, items, columns)

    layer_sums = [None] * layers
    scale_grads = [None] * layers
    mod_sums = [[None] * 6 for _ in range(layers)]
    grad_low, sums = first_back(grad_carried, *saved[-1][-1], mods[-1], here_member, choose, 1)
    mod_sums[-1][1] = (sums, 0)
    for layer in range(layers - 1, -1, -1):
        qkv_full, proj_full, fc1_full, fc2_full = weights[layer]
        carried_in, middle, first, kept, attended, second, slope, activated, branch = saved[layer]
        other = across_cores(grad_low)
        if near and layer == 0:
            other = tie(other, layer_sums[1][1].arrived)
            other = layer_sums[1][1].fold(True, other)
        grad_branch = (grad_low, other)
        if near:
            terms = gradients((activated, grad_branch))
            sums_fc2 = Sums(*terms)
            slope = tie(slope, *terms)
        part_own, part_a, part_b, grad_hidden = mlp_back(*grad_branch, slope, fc1_full, fc2_full)
        here, there = sum_pack_rows(part_own, (part_a, part_b))
        if near:
            terms = gradients((tie(grad_hidden, here), second))
            sums_fc1 = Sums(*terms)
            there = tie(there, *terms, *([layer_sums[1][2].blocks, layer_sums[1][0].arrived] if layer == 0 else [mixed_out]))
            if layer == 0:
                there = layer_sums[1][0].fold(True, there)
        else:
            sums_fc2 = WholeSums(gradient_blocks(order, (activated, grad_branch)))
            sums_fc1 = WholeSums(gradient_blocks(order, (grad_hidden, second)))
        grad_middle, grad_low, sums = step_back(
            middle, here, there, grad_carried, mods[layer], here_member, choose, 3, (mods[layer], 0, *attended)
        )
        mod_sums[layer][3], mod_sums[layer][5], mod_sums[layer][0] = ((sums, i * width) for i in range(3))
        other = across_cores(grad_low)
        if near and layer == 0:
            other = tie(other, layer_sums[1][1].blocks)
        grad_attended = (grad_low, other)
        part_own, part_a, part_b, grad_projected, scale_grads[layer] = attend_back(
            *grad_attended, kept, qkv_full, proj_full, scales[layer], layout, heads_here
        )
        if near and layer == 0:
            terms = gradients(((kept[0], 3 * span, 4 * span), grad_attended), (grad_projected, first))
            part_a = tie(part_a, *terms, sums_fc2.arrived)
            part_a = sums_fc2.fold(True, part_a)
        elif near:
            part_a = tie(part_a, sums_fc2.arrived)
            part_a = sums_fc2.fold(True, part_a)
        here, there = sum_pack_rows(part_own, (part_a, part_b))
        if near:
            if layer > 0:
                terms = gradients(((tie(kept[0], here), 3 * span, 4 * span), grad_attended), (grad_projected, first))
            there = tie(there, *terms)
            if layer == 0:
                there = tie(there, sums_fc1.arrived, layer_sums[1][0].blocks)
                there = sums_fc1.fold(True, there)
            sums_attn = Sums(*terms)
        else:
            sums_attn = WholeSums(gradient_blocks(order, (kept[0][:, 3 * span :], grad_attended), (grad_projected, first)))
        if layer > 0:
            grad_carried, grad_low, sums = step_back(
                carried_in, here, there, grad_middle, mods[layer], here_member, choose, 2, (mods[layer - 1], 1, *saved[layer - 1][-1])
            )
            mod_sums[layer - 1][1] = (sums, 2 * width)
        else:
            grad_carried, sums = step_back(carried_in, here, there, grad_middle, mods[layer], here_member, choose, 2)
        mod_sums[layer][2], mod_sums[layer][4] = (sums, 0), (sums, width)
        layer_sums[layer] = (sums_attn, sums_fc1, sums_fc2)
    if near:
        grad_carried = tie(grad_carried, layer_sums[0][0].arrived)

    grads_back = repack(to_rows, grad_carried, order).reshape(groups, slots, width)
    sent = jnp.stack([give(layer) for layer in range(layers)], axis=1).reshape(groups, layers * items * columns)
    if sent.shape[1] % width:
        back = exchange(jnp.concatenate([mixed_out, grads_back], axis=1), groups)
        mods_back = exchange(sent, groups)
    else:
        sent = sent.reshape(groups, -1, width)
        back = exchange(jnp.concatenate([mixed_out, grads_back, sent], axis=1), groups)
        mods_back = back[:, 2 * slots :]
    mixed_back, grads_back = back[:, :slots], back[:, slots : 2 * slots]
    mods_back = mods_back.reshape(groups, layers, items, columns)
    if near:
        mods_back = tie(mods_back, layer_sums[0][1].blocks)
    mods_back = [mods_back[:, layer] for layer in range(layers)]

    mixed = contract_rows(to_slots, mixed_back.reshape(rows, width)).astype(low)
    tokens_grad = contract_rows(to_slots, grads_back.reshape(rows, width)).astype(low)
    ada_grad, grad_silu = condition_back(
        cond, w_ada, [back.reshape(groups * items, columns) for back in mods_back]
    )
    logs = jnp.pad(jnp.stack(scale_grads).reshape(1, -1), ((0, 7), (0, cond.shape[1] - layers * heads_here)))
    summed = jnp.concatenate([grad_silu, logs], axis=0)
    if paired(groups):
        for offset in (1, 2, 4):
            summed = summed + swap(summed, "dp", offset)
            if offset == 2:
                layer_sums[0][0].fold(False, summed)
    else:
        summed = lax.psum(summed, "dp")
    grad_silu = summed[: cond.shape[0]]
    scale_grad = summed[cond.shape[0], : layers * heads_here].reshape(layers, heads_here)
    table_grad = table_back(all_classes[None, :], cond, grad_silu, class_table.shape[0])
    spanned = w_proj.shape[1]
    layer_grads = []
    for layer in range(layers):
        attn, fc1, fc2 = (sums.total(scale_grad) for sums in layer_sums[layer])
        layer_grads.append((attn[spanned:].T.reshape(w_qkv.shape[1:]), attn[:spanned], fc1.T, fc2))
    qkv_grad, proj_grad, fc1_grad, fc2_grad = (
        jnp.stack([layer_grads[layer][i] for layer in range(layers)]) for i in range(4)
    )
    return (
        mixed,
        tokens_grad,
        table_grad,
        ada_grad,
        qkv_grad,
        scale_grad,
        proj_grad,
        fc1_grad,
        fc2_grad,
    )


def solution(mesh):
    placed = (
        P(("dp", "shard"), None),
        P(("dp", "shard"), None),
        P(None, "shard", None),
        P("dp", None),
        P("dp", None),
        P(None, "shard"),
        P(None, "shard", "dp"),
        P(None, "dp", None, "shard"),
        P(None, "shard"),
        P(None, "shard", "dp"),
        P(None, "dp", "shard"),
        P(None, "shard", "dp"),
    )
    return jax.shard_map(
        on_device,
        mesh=mesh,
        in_specs=placed,
        out_specs=(
            P(("dp", "shard"), None),
            P(("dp", "shard"), None),
            P(None, "shard"),
            P(None, "shard", "dp"),
            P(None, "dp", None, "shard"),
            P(None, "shard"),
            P(None, "shard", "dp"),
            P(None, "dp", "shard"),
            P(None, "shard", "dp"),
        ),
        check_vma=False,
    )
```
